128 devices in a mesh: member: 32 (over y_hi, x, z), space: 4 (over y_lo, core).
Axes of the slice: x: 4, y: 4 (y_hi: 2, y_lo: 2; y = y_hi * 2 + y_lo), z: 4, core: 2. Of those that a mesh axis runs over, the one named last changes fastest.
Arguments:
- states: float32 [1024, 98304], P('member', 'space'), may hold values from -6 to 6
- obs_values: float32 [2, 2048], replicated, may hold values from -6 to 6
- obs_weights: float32 [2, 2048], replicated, may hold values from 0.2 to 2
- obs_cell: int32 [2, 4, 4], P(None, 'space'), may hold values from 0 to 191
- op_select: int32 [2, 4, 4], P(None, 'space'), may hold values from 0 to 7
- op_table: float32 [8, 128, 128], replicated, may hold values from -0.5 to 0.5
- loc_obs: int32 [2, 4, 192, 8], P(None, 'space', 'member'), may hold values from 0 to 11
- loc_tile: int32 [2, 4, 192, 8], P(None, 'space', 'member'), may hold values from 0 to 7
- loc_tiles: float32 [8, 128, 128], replicated, may hold values from 0 to 1
Outputs:
- analysis: float32 [1024, 98304], P('member', 'space')
The draws below stay inside these ranges and needn't reach their ends.
All inputs are finite; a program needn't handle non-finite values.
Results may differ from the reference program's by a relative error of at most 0.00012.
Values sent between devices are 32-bit elements; how exact they have to be, the bound alone decides.
No kernel may reach another device: no remote copies, remote signals or barrier semaphores. Data moves between devices by JAX's collectives and lax.ppermute only.
A program may use at most 128 MiB of HBM per device.

```python
import math
import jax
import jax.numpy as jnp
from jax import lax

K = 1024
BLK = 128
OB = 4
LOC = 8
NH = 8
NT = 8
BATCHES = 2
NB = 192
NCELLS = 98304
NOB = 16
N_SPACE = 4


def plant(entries, stream_key, smallest, largest):
    shape = entries.shape
    place = [jax.random.randint(jax.random.fold_in(stream_key, axis), (), 0, shape[axis]) for axis in range(len(shape))]
    entries = entries.at[tuple(place)].set(smallest)
    longest = shape.index(max(shape))
    place[longest] = (place[longest] + 1) % shape[longest]
    return entries.at[tuple(place)].set(largest)


def block_levels(stream_key, dims, shards, smallest, largest):
    def one(axis_at, blocks):
        heights = jax.random.uniform(jax.random.fold_in(jax.random.fold_in(stream_key, 6), axis_at), (blocks,), jnp.float32, smallest / len(shards), largest / len(shards))
        return jnp.repeat(jnp.exp(heights), dims[axis_at] // blocks).reshape((-1,) + (1,) * (len(dims) - axis_at - 1))

    level = one(*shards[0])
    for cut in shards[1:]:
        level = level * one(*cut)
    return level


def scatter_about(stream_key, extent, scale, bound, shards=(), dtype=jnp.bfloat16):
    factor_of = block_levels(stream_key, extent, shards, -0.22, 0.18) if shards else 1.0
    entries = jax.random.normal(stream_key, extent, jnp.float32) * scale * factor_of
    return jnp.minimum(jnp.maximum(entries, -bound), bound).astype(dtype)


def setup_inputs(seed: int = 0) -> dict:
    splits = jax.random.split(jax.random.key(seed), 10)
    return {
        "states": scatter_about(splits[0], (K, NCELLS), 1.0, 6.0, ((0, 32), (1, 4)), jnp.float32),
        "obs_values": scatter_about(splits[1], (BATCHES, NOB * BLK), 1.0, 6.0, (), jnp.float32),
        "obs_weights": jnp.clip(jnp.exp(jax.random.uniform(splits[2], (BATCHES, NOB * BLK), jnp.float32, math.log(0.2), math.log(2.0))), 0.2, 2.0),
        "obs_cell": plant(jax.random.randint(splits[3], (BATCHES, N_SPACE, OB), 0, NB), jax.random.fold_in(splits[3], 1), 0, NB - 1).astype(jnp.int32),
        "op_select": plant(jax.random.randint(splits[4], (BATCHES, N_SPACE, OB), 0, NH), jax.random.fold_in(splits[4], 1), 0, NH - 1).astype(jnp.int32),
        "op_table": scatter_about(splits[5], (NH, BLK, BLK), BLK ** -0.5, 0.5, (), jnp.float32),
        "loc_obs": plant(jax.random.randint(splits[6], (BATCHES, N_SPACE, NB, LOC), 0, 3 * OB), jax.random.fold_in(splits[6], 1), 0, (3 * OB) - 1).astype(jnp.int32),
        "loc_tile": plant(jax.random.randint(splits[7], (BATCHES, N_SPACE, NB, LOC), 0, NT), jax.random.fold_in(splits[7], 1), 0, NT - 1).astype(jnp.int32),
        "loc_tiles": jnp.clip(jax.random.uniform(splits[8], (NT, BLK, BLK), jnp.float32, 0.0, 1.0), 0.0, 1.0),
    }


def observe(blocks, obs_cell, op_select, op_table, batch_no):
    parts = []
    for slab_no in range(N_SPACE):
        picked = blocks[:, slab_no][:, obs_cell[batch_no, slab_no]]
        operators = op_table[op_select[batch_no, slab_no]]
        parts.append(jnp.einsum("koc,opc->kop", picked, operators, precision=lax.Precision.HIGHEST))
    return jnp.concatenate(parts, axis=1)


def reference(states, obs_values, obs_weights, obs_cell, op_select, op_table, loc_obs, loc_tile, loc_tiles):
    ensemble = states.reshape(K, N_SPACE, NB, BLK)
    for batch_no in range(BATCHES):
        observed = observe(ensemble, obs_cell, op_select, op_table, batch_no)
        obs_mean = jnp.mean(observed, axis=0)
        obs_anom = observed - obs_mean
        values = obs_values[batch_no].reshape(NOB, BLK)
        weights = obs_weights[batch_no].reshape(NOB, BLK)
        innov = weights * (values - obs_mean) - 0.5 * weights * obs_anom
        state_mean = jnp.mean(ensemble, axis=0)
        slabs = []
        for slab_no in range(N_SPACE):
            order = [(slab_no - 1) % N_SPACE, slab_no, (slab_no + 1) % N_SPACE]
            anom_win = jnp.concatenate([obs_anom[:, q * OB:(q + 1) * OB] for q in order], axis=1)
            innov_win = jnp.concatenate([innov[:, q * OB:(q + 1) * OB] for q in order], axis=1)

            def update_block(packed):
                cell_blk, mean_blk, reach, tile_pick = packed
                state_anom = cell_blk - mean_blk
                chosen = anom_win[:, reach]
                covariance = jnp.einsum("kc,klo->lco", state_anom, chosen, precision=lax.Precision.HIGHEST) / (K - 1)
                gain = loc_tiles[tile_pick] * covariance
                increment = jnp.einsum("klo,lco->kc", innov_win[:, reach], gain, precision=lax.Precision.HIGHEST)
                return cell_blk + increment

            fresh = lax.map(update_block, (ensemble[:, slab_no].transpose(1, 0, 2), state_mean[slab_no], loc_obs[batch_no, slab_no], loc_tile[batch_no, slab_no]))
            slabs.append(fresh.transpose(1, 0, 2))
        ensemble = jnp.stack(slabs, axis=1)
    return ensemble.reshape(K, NCELLS)
```

```python
import functools

import jax
import jax.numpy as jnp
from jax import lax
from jax.experimental import pallas as pl
from jax.experimental.pallas import tpu as pltpu
from jax.sharding import PartitionSpec as P

K = 1024
BLK = 128
OB = 4
LOC = 8
BATCHES = 2
MEMBERS = 32
CB_DEV = 6
WIN = 3 * OB
PAD = 16
VMEM_BYTES = 60 * 1024 * 1024

F32 = jnp.float32
BF16 = jnp.bfloat16
PARAMS = pltpu.CompilerParams(vmem_limit_bytes=VMEM_BYTES)


def split_high_low(value):
    high = value.astype(BF16)
    low = (value - high.astype(F32)).astype(BF16)
    return high, low


def dot_nn(a, b):
    return lax.dot_general(a, b, (((1,), (0,)), ((), ())), preferred_element_type=F32)


def dot_nt(a, b, precision=None):
    return lax.dot_general(
        a, b, (((1,), (1,)), ((), ())), preferred_element_type=F32, precision=precision
    )


def observe_kernel(cell_ref, op_ref, *refs):
    first, second, ops = refs[:OB], refs[OB : 2 * OB], refs[2 * OB : 3 * OB]
    observed_ref, raw_ref = refs[3 * OB :]
    for o in range(OB):
        cols = slice(o * BLK, (o + 1) * BLK)
        observed_ref[:, cols] = dot_nt(first[o][...], ops[o][0], lax.Precision.HIGHEST)
        raw_ref[:, cols] = second[o][...]


def observe_members(states, obs_cell, op_select, op_table):
    members = states.shape[0]

    def cells_of(batch, o):
        return pl.BlockSpec((members, BLK), lambda i, cell, op: (0, cell[batch, o]))

    def operator_of(o):
        return pl.BlockSpec((1, BLK, BLK), lambda i, cell, op: (op[0, o], 0, 0))

    whole = pl.BlockSpec((members, OB * BLK), lambda i, cell, op: (0, 0))
    shape = jax.ShapeDtypeStruct((members, OB * BLK), F32)
    return pl.pallas_call(
        observe_kernel,
        grid_spec=pltpu.PrefetchScalarGridSpec(
            num_scalar_prefetch=2,
            grid=(1,),
            in_specs=[cells_of(b, o) for b in range(BATCHES) for o in range(OB)]
            + [operator_of(o) for o in range(OB)],
            out_specs=[whole, whole],
        ),
        out_shape=[shape, shape],
        compiler_params=PARAMS,
        name="observe",
    )(obs_cell, op_select, *([states] * (2 * OB)), *([op_table] * OB))


def tiles_kernel(obs_ref, tile_ref, tiles_ref, weights_ref, out_ref):
    n = pl.program_id(0)
    out_ref[...] = jnp.zeros_like(out_ref)
    for l in range(LOC):
        j = pl.multiple_of(obs_ref[n, l] * BLK, BLK)
        out_ref[:, pl.ds(j, BLK)] += tiles_ref[tile_ref[n, l]]
    out_ref[...] = out_ref[...] * (weights_ref[0] * (-0.5 / (K - 1)))


def weighted_tiles(loc_obs, loc_tile, loc_tiles, weights):
    blocks = loc_obs.shape[0]
    return pl.pallas_call(
        tiles_kernel,
        grid_spec=pltpu.PrefetchScalarGridSpec(
            num_scalar_prefetch=2,
            grid=(blocks,),
            in_specs=[
                pl.BlockSpec(loc_tiles.shape, lambda n, a, b: (0, 0, 0)),
                pl.BlockSpec(
                    (1, 1, WIN * BLK),
                    lambda n, a, b: (jnp.where((n >= CB_DEV) & (n < 2 * CB_DEV), 1, 0), 0, 0),
                ),
            ],
            out_specs=pl.BlockSpec((BLK, WIN * BLK), lambda n, a, b: (n, 0)),
        ),
        out_shape=jax.ShapeDtypeStruct((blocks * BLK, WIN * BLK), F32),
        compiler_params=PARAMS,
        name="weighted_tiles",
    )(loc_obs, loc_tile, loc_tiles, weights.reshape(BATCHES, 1, WIN * BLK))


def split_observed(y_ref, first, count, values_ref, yh, yl):
    for b in range(count):
        src = slice(b * BLK, (b + 1) * BLK)
        dst = slice((first + b) * BLK, (first + b + 1) * BLK)
        y = y_ref[:, src]
        mean = jnp.sum(y, axis=0, keepdims=True) * (1.0 / K)
        yh[0:K, dst], yl[0:K, dst] = split_high_low(y - mean)
        shift = jnp.broadcast_to(-2.0 * (values_ref[:, dst] - mean), (PAD, BLK))
        yh[K : K + PAD, dst], yl[K : K + PAD, dst] = split_high_low(shift)


def split_cells(x_ref, col0, nb, xh, xl):
    for n in range(nb):
        x = x_ref[:, col0 + n * BLK : col0 + (n + 1) * BLK]
        anom = x - jnp.sum(x, axis=0, keepdims=True) * (1.0 / K)
        rows = slice(n * BLK, (n + 1) * BLK)
        xh[rows, :], xl[rows, :] = split_high_low(anom.T)


def gains(tiles_ref, xh, xl, yh, yl, gh, gl):
    wide = 2 * BLK

    @pl.loop(0, WIN // 2)
    def _(j):
        cols = pl.ds(pl.multiple_of(j * wide, wide), wide)
        high, low = yh[0:K, cols], yl[0:K, cols]
        cov = dot_nn(xh[...], high) + dot_nn(xh[...], low) + dot_nn(xl[...], high)
        gh[:, cols], gl[:, cols] = split_high_low(cov * tiles_ref[:, cols])


def add_increment(nb, x_ref, col0, out_ref, yh, yl, gh, gl):
    wide = 2 * BLK
    for n in range(nb // 2):
        rows = slice(n * wide, (n + 1) * wide)
        high, low = gh[rows, :], gl[rows, :]
        inc = dot_nt(yh[...], high) + dot_nt(yh[...], low) + dot_nt(yl[...], high)
        x = x_ref[:, col0 + n * wide : col0 + (n + 1) * wide]
        out_ref[:, n * wide : (n + 1) * wide] = x + inc[0:K] + inc[K : K + 1]


def update_kernel(widths, nb, x_ref, *refs):
    y_refs = refs[: len(widths)]
    tiles_ref, values_ref, out_ref, xh, xl, yh, yl, gh, gl = refs[len(widths) :]
    first = 0
    for y_ref, count in zip(y_refs, widths):
        split_observed(y_ref, first, count, values_ref, yh, yl)
        first += count
    split_cells(x_ref, 0, nb, xh, xl)
    gains(tiles_ref, xh, xl, yh, yl, gh, gl)
    add_increment(nb, x_ref, 0, out_ref, yh, yl, gh, gl)


def work_arrays(nb):
    return [
        pltpu.VMEM((nb * BLK, K), BF16),
        pltpu.VMEM((nb * BLK, K), BF16),
        pltpu.VMEM((K + PAD, WIN * BLK), BF16),
        pltpu.VMEM((K + PAD, WIN * BLK), BF16),
        pltpu.VMEM((nb * BLK, WIN * BLK), BF16),
        pltpu.VMEM((nb * BLK, WIN * BLK), BF16),
    ]


def update_cells(cells, observed, widths, tiles, tiles_at, values, batch_no):
    nb = CB_DEV
    return pl.pallas_call(
        functools.partial(update_kernel, widths, nb),
        grid=(1,),
        in_specs=[pl.BlockSpec((K, nb * BLK), lambda i: (0, 0))]
        + [pl.BlockSpec((K, w * BLK), lambda i: (0, 0)) for w in widths]
        + [
            pl.BlockSpec((nb * BLK, WIN * BLK), lambda i: (tiles_at, 0)),
            pl.BlockSpec((1, WIN * BLK), lambda i: (0, 0)),
        ],
        out_specs=pl.BlockSpec((K, nb * BLK), lambda i: (0, 0)),
        out_shape=jax.ShapeDtypeStruct((K, nb * BLK), F32),
        scratch_shapes=work_arrays(nb),
        compiler_params=PARAMS,
        cost_estimate=pl.CostEstimate(
            flops=12 * K * nb * BLK * WIN * BLK, bytes_accessed=18 << 20, transcendentals=0
        ),
        name=f"update_cells_{batch_no}",
    )(cells, *observed, tiles, values)


def observe_all_kernel(op_ref, all_ref, tiles_ref, values_ref, table_ref, out_ref, *work):
    xh, xl, yh, yl, gh, gl = work
    split_observed(all_ref, 0, WIN, values_ref, yh, yl)
    split_cells(all_ref, WIN * BLK, OB, xh, xl)
    gains(tiles_ref, xh, xl, yh, yl, gh, gl)
    add_increment(OB, all_ref, WIN * BLK, out_ref, yh, yl, gh, gl)
    for o in range(OB):
        cols = slice(o * BLK, (o + 1) * BLK)
        operator = table_ref[op_ref[1, o]]
        out_ref[:, cols] = dot_nt(out_ref[:, cols], operator, lax.Precision.HIGHEST)


def observe_all(gathered, tiles, values, op_select, op_table):
    return pl.pallas_call(
        observe_all_kernel,
        grid_spec=pltpu.PrefetchScalarGridSpec(
            num_scalar_prefetch=1,
            grid=(1,),
            in_specs=[
                pl.BlockSpec((K, (WIN + OB) * BLK), lambda i, op: (0, 0)),
                pl.BlockSpec((OB * BLK, WIN * BLK), lambda i, op: (BATCHES * CB_DEV // OB, 0)),
                pl.BlockSpec((1, WIN * BLK), lambda i, op: (0, 0)),
                pl.BlockSpec(op_table.shape, lambda i, op: (0, 0, 0)),
            ],
            out_specs=pl.BlockSpec((K, OB * BLK), lambda i, op: (0, 0)),
            scratch_shapes=work_arrays(OB),
        ),
        out_shape=jax.ShapeDtypeStruct((K, OB * BLK), F32),
        compiler_params=PARAMS,
        cost_estimate=pl.CostEstimate(
            flops=12 * K * OB * BLK * WIN * BLK, bytes_accessed=14 << 20, transcendentals=0
        ),
        name="observe_all",
    )(op_select, gathered, tiles, values, op_table)


def neighbour_slabs(value):
    up, down = [], []
    for member in range(MEMBERS):
        y_hi, rest = member // 16, member % 16
        for slab in range(4):
            y_lo, core = slab // 2, slab % 2
            y = y_hi * 2 + y_lo

            def index(y_pos, core_no):
                y_pos = y_pos % 4
                return ((y_pos // 2) * 16 + rest) * 4 + (y_pos % 2) * 2 + core_no

            here = index(y, core)
            up.append((here, index(y, 1) if core == 0 else index(y + 1, 0)))
            down.append((here, index(y, 0) if core == 1 else index(y - 1, 1)))
    both = ("member", "space")
    return lax.ppermute(value, both, up), lax.ppermute(value, both, down)


def window_rows(rows):
    count = lax.axis_size("space")
    slab = lax.axis_index("space")
    by_slab = rows.reshape(BATCHES, count, OB * BLK)
    pick = (slab - 1 + jnp.arange(3, dtype=jnp.int32)) % count
    return by_slab[:, pick].reshape(BATCHES, WIN * BLK)


def per_device(
    states, obs_values, obs_weights, obs_cell, op_select, op_table, loc_obs, loc_tile, loc_tiles
):
    obs_cell, op_select = obs_cell[:, 0], op_select[:, 0]
    loc_obs, loc_tile = loc_obs[:, 0], loc_tile[:, 0]

    observed, raw = observe_members(states, obs_cell, op_select, op_table)
    ring = [(i, (i + 1) % 4) for i in range(4)]
    back = [((i + 1) % 4, i) for i in range(4)]
    near = jnp.concatenate(
        [
            lax.ppermute(observed, "space", ring),
            observed,
            lax.ppermute(observed, "space", back),
            raw,
        ],
        axis=1,
    )
    gathered = lax.all_gather(near, "member", axis=0, tiled=True)

    cells = lax.all_to_all(states, "member", split_axis=1, concat_axis=0, tiled=True)

    loc = jnp.concatenate([loc_obs[0], loc_tile[0]], axis=1)
    loc = jnp.pad(loc, ((0, 8 - CB_DEV), (0, BLK - 2 * LOC)))
    loc = lax.all_to_all(
        jnp.broadcast_to(loc[None], (MEMBERS, 8, BLK)), "member", 0, 0, tiled=True
    )
    loc = loc[:, :CB_DEV, : 2 * LOC].reshape(MEMBERS * CB_DEV, 2 * LOC)[obs_cell[1]]

    values, weights = window_rows(obs_values), window_rows(obs_weights)
    tiles = weighted_tiles(
        jnp.concatenate([loc_obs[0], loc_obs[1], loc[:, :LOC]], axis=0),
        jnp.concatenate([loc_tile[0], loc_tile[1], loc[:, LOC:]], axis=0),
        loc_tiles,
        weights,
    )

    observed = observe_all(gathered, tiles, values[:1], op_select, op_table)
    before, after = neighbour_slabs(observed)
    cells = update_cells(cells, (gathered,), (WIN,), tiles, 0, values[:1], 0)
    cells = update_cells(
        cells, (before, observed, after), (OB, OB, OB), tiles, 1, values[1:], 1
    )
    return lax.all_to_all(cells, "member", split_axis=0, concat_axis=1, tiled=True)


def solution(mesh):
    placed = (
        P("member", "space"),
        P(),
        P(),
        P(None, "space", None),
        P(None, "space", None),
        P(),
        P(None, "space", "member", None),
        P(None, "space", "member", None),
        P(),
    )
    return jax.shard_map(
        per_device, mesh=mesh, in_specs=placed, out_specs=P("member", "space"), check_vma=False
    )
```

```python
import functools

import jax
import jax.numpy as jnp
from jax import lax
from jax.experimental import pallas as pl
from jax.experimental.pallas import tpu as pltpu
from jax.sharding import PartitionSpec as P

K = 1024
BLK = 128
OB = 4
LOC = 8
BATCHES = 2
MEMBERS = 32
CB_DEV = 6
WIN = 3 * OB
PAD = 16
VMEM_BYTES = 60 * 1024 * 1024

F32 = jnp.float32
BF16 = jnp.bfloat16
PARAMS = pltpu.CompilerParams(vmem_limit_bytes=VMEM_BYTES)


def split_high_low(value):
    high = value.astype(BF16)
    low = (value - high.astype(F32)).astype(BF16)
    return high, low


def dot_nn(a, b):
    return lax.dot_general(a, b, (((1,), (0,)), ((), ())), preferred_element_type=F32)


def dot_nt(a, b, precision=None):
    return lax.dot_general(
        a, b, (((1,), (1,)), ((), ())), preferred_element_type=F32, precision=precision
    )


def observe_kernel(cell_ref, op_ref, *refs):
    first, second, ops = refs[:OB], refs[OB : 2 * OB], refs[2 * OB : 3 * OB]
    observed_ref, raw_ref = refs[3 * OB :]
    for o in range(OB):
        cols = slice(o * BLK, (o + 1) * BLK)
        observed_ref[:, cols] = dot_nt(first[o][...], ops[o][0], lax.Precision.HIGHEST)
        raw_ref[:, cols] = second[o][...]


def observe_members(states, obs_cell, op_select, op_table):
    members = states.shape[0]

    def cells_of(batch, o):
        return pl.BlockSpec((members, BLK), lambda i, cell, op: (0, cell[batch, o]))

    def operator_of(o):
        return pl.BlockSpec((1, BLK, BLK), lambda i, cell, op: (op[0, o], 0, 0))

    whole = pl.BlockSpec((members, OB * BLK), lambda i, cell, op: (0, 0))
    shape = jax.ShapeDtypeStruct((members, OB * BLK), F32)
    return pl.pallas_call(
        observe_kernel,
        grid_spec=pltpu.PrefetchScalarGridSpec(
            num_scalar_prefetch=2,
            grid=(1,),
            in_specs=[cells_of(b, o) for b in range(BATCHES) for o in range(OB)]
            + [operator_of(o) for o in range(OB)],
            out_specs=[whole, whole],
        ),
        out_shape=[shape, shape],
        compiler_params=PARAMS,
        name="observe",
    )(obs_cell, op_select, *([states] * (2 * OB)), *([op_table] * OB))


def tiles_kernel(obs_ref, tile_ref, tiles_ref, weights_ref, out_ref):
    n = pl.program_id(0)
    out_ref[...] = jnp.zeros_like(out_ref)
    for l in range(LOC):
        cols = pl.ds(pl.multiple_of(obs_ref[n, l] * BLK, BLK), BLK)
        scale = weights_ref[0, :, cols] * (-0.5 / (K - 1))
        out_ref[:, cols] += tiles_ref[tile_ref[n, l]] * scale


def weighted_tiles(loc_obs, loc_tile, loc_tiles, weights):
    blocks = loc_obs.shape[0]
    return pl.pallas_call(
        tiles_kernel,
        grid_spec=pltpu.PrefetchScalarGridSpec(
            num_scalar_prefetch=2,
            grid=(blocks,),
            in_specs=[
                pl.BlockSpec(loc_tiles.shape, lambda n, a, b: (0, 0, 0)),
                pl.BlockSpec(
                    (1, 1, WIN * BLK),
                    lambda n, a, b: (jnp.where((n >= CB_DEV) & (n < 2 * CB_DEV), 1, 0), 0, 0),
                ),
            ],
            out_specs=pl.BlockSpec((BLK, WIN * BLK), lambda n, a, b: (n, 0)),
        ),
        out_shape=jax.ShapeDtypeStruct((blocks * BLK, WIN * BLK), F32),
        compiler_params=PARAMS,
        cost_estimate=pl.CostEstimate(flops=1 << 22, bytes_accessed=14 << 20, transcendentals=0),
        name="weighted_tiles",
    )(loc_obs, loc_tile, loc_tiles, weights.reshape(BATCHES, 1, WIN * BLK))


CHUNK = 2 * BLK
SLAB = OB * BLK
ROWS = 32
ANY = pl.BlockSpec(memory_space=pl.ANY)
SMEM = pl.BlockSpec(memory_space=pltpu.SMEM)
VMEM = pl.BlockSpec(memory_space=pltpu.VMEM)


def chunk(number):
    return slice(number * CHUNK, (number + 1) * CHUNK)


def split_observed(y_ref, src, dst, values_ref, yh, yl):
    y = y_ref[:, chunk(src)]
    mean = jnp.sum(y, axis=0, keepdims=True) * (1.0 / K)
    yh[0:K, chunk(dst)], yl[0:K, chunk(dst)] = split_high_low(y - mean)
    shift = jnp.broadcast_to(-2.0 * (values_ref[:, chunk(dst)] - mean), (PAD, CHUNK))
    yh[K : K + PAD, chunk(dst)], yl[K : K + PAD, chunk(dst)] = split_high_low(shift)


def split_cells(x_ref, col0, nb, xh, xl):
    for n in range(nb):
        x = x_ref[:, col0 + n * BLK : col0 + (n + 1) * BLK]
        anom = x - jnp.sum(x, axis=0, keepdims=True) * (1.0 / K)
        rows = slice(n * BLK, (n + 1) * BLK)
        xh[rows, :], xl[rows, :] = split_high_low(anom.T)


def gains(cols, tile_cols, tiles_ref, xh, xl, yh, yl, gh, gl):
    high, low = yh[0:K, cols], yl[0:K, cols]
    cov = dot_nn(xh[...], high) + dot_nn(xh[...], low) + dot_nn(xl[...], high)
    gh[:, cols], gl[:, cols] = split_high_low(cov * tiles_ref[:, tile_cols])


def increment(number, yh, yl, gh, gl):
    high, low = gh[chunk(number), :], gl[chunk(number), :]
    inc = dot_nt(yh[...], high) + dot_nt(yh[...], low) + dot_nt(yl[...], high)
    return inc[0:K] + inc[K : K + 1]


def bf16_pair(rows, cols):
    return [jax.ShapeDtypeStruct((rows, cols), BF16)] * 2


def vmem_pair(rows, cols):
    return [pltpu.VMEM((rows, cols), BF16)] * 2


def copies(sems, pairs):
    out = [pltpu.make_async_copy(src, dst, sems.at[i]) for i, (src, dst) in enumerate(pairs)]
    for copy in out:
        copy.start()
    return out


CELLS = CB_DEV * BLK
WINDOW = WIN * BLK
OWN = slice(SLAB, 2 * SLAB)


def update_first_kernel(
    values_ref, x_in, yh_in, yl_in, own_in, t_first, t_second,
    x_out, xh_out, xl_out, yh_out, yl_out, gh_out, gl_out,
    x, yh, yl, own, t1, t2, xh, xl, gh, gl, y2h, y2l, g2h, g2l, sems,
):
    x_load, yh_load, yl_load, t1_load, own_load, t2_load = copies(
        sems,
        [
            (x_in, x),
            (yh_in, yh),
            (yl_in, yl),
            (t_first.at[0:CELLS, :], t1),
            (own_in, own),
            (t_second.at[CELLS : 2 * CELLS, OWN], t2),
        ],
    )
    x_load.wait()
    split_cells(x, 0, CB_DEV, xh, xl)
    yh_load.wait()
    yl_load.wait()
    t1_load.wait()
    for number in range(WINDOW // CHUNK):
        gains(chunk(number), chunk(number), t1, xh, xl, yh, yl, gh, gl)
    for number in range(CELLS // CHUNK):
        x[:, chunk(number)] += increment(number, yh, yl, gh, gl)
    split_cells(x, 0, CB_DEV, xh, xl)
    own_load.wait()
    t2_load.wait()
    stores = []

    def store(source, target):
        stores.append(pltpu.make_async_copy(source, target, sems.at[6 + len(stores)]))
        stores[-1].start()

    store(x, x_out)
    store(xh, xh_out)
    store(xl, xl_out)
    for number in range(SLAB // CHUNK):
        split_observed(own, number, number, values_ref, y2h, y2l)
        gains(chunk(number), chunk(number), t2, xh, xl, y2h, y2l, g2h, g2l)
    store(y2h, yh_out)
    store(y2l, yl_out)
    store(g2h, gh_out)
    store(g2l, gl_out)
    for copy in stores:
        copy.wait()


def update_first(cells, yh, yl, own, tiles, values):
    return pl.pallas_call(
        update_first_kernel,
        in_specs=[VMEM] + [ANY] * 6,
        out_specs=[ANY] * 7,
        out_shape=[jax.ShapeDtypeStruct((K, CELLS), F32)]
        + bf16_pair(CELLS, K)
        + bf16_pair(K + PAD, SLAB)
        + bf16_pair(CELLS, SLAB),
        scratch_shapes=[pltpu.VMEM((K, CELLS), F32)]
        + vmem_pair(K + PAD, WINDOW)
        + [
            pltpu.VMEM((K, SLAB), F32),
            pltpu.VMEM((CELLS, WINDOW), F32),
            pltpu.VMEM((CELLS, SLAB), F32),
        ]
        + vmem_pair(CELLS, K)
        + vmem_pair(CELLS, WINDOW)
        + vmem_pair(K + PAD, SLAB)
        + vmem_pair(CELLS, SLAB)
        + [pltpu.SemaphoreType.DMA((13,))],
        compiler_params=PARAMS,
        cost_estimate=pl.CostEstimate(
            flops=14 * K * CELLS * WINDOW, bytes_accessed=25 << 20, transcendentals=0
        ),
        name="update_first",
    )(values[:, OWN], cells, yh, yl, own, tiles, tiles)


def update_second_kernel(
    values_ref, x_in, xh_in, xl_in, yh_in, yl_in, gh_in, gl_in, before_in, after_in, t_in,
    x_out,
    x, xh, xl, yh, yl, gh, gl, y, tiles, sems,
):
    loads = copies(
        sems,
        [
            (before_in, y.at[:, 0:SLAB]),
            (xh_in, xh),
            (xl_in, xl),
            (t_in.at[CELLS : 2 * CELLS, :], tiles),
            (after_in, y.at[:, SLAB : 2 * SLAB]),
            (yh_in, yh.at[:, OWN]),
            (yl_in, yl.at[:, OWN]),
            (gh_in, gh.at[:, OWN]),
            (gl_in, gl.at[:, OWN]),
            (x_in, x),
        ],
    )
    per = SLAB // CHUNK
    for load in loads[:4]:
        load.wait()
    for number in range(per):
        split_observed(y, number, number, values_ref, yh, yl)
        gains(chunk(number), chunk(number), tiles, xh, xl, yh, yl, gh, gl)
    loads[4].wait()
    for number in range(per):
        split_observed(y, per + number, 2 * per + number, values_ref, yh, yl)
        cols = chunk(2 * per + number)
        gains(cols, cols, tiles, xh, xl, yh, yl, gh, gl)
    for load in loads[5:]:
        load.wait()
    stores = []
    for number in range(CELLS // CHUNK):
        x[:, chunk(number)] += increment(number, yh, yl, gh, gl)
        stores.append(
            pltpu.make_async_copy(
                x.at[:, chunk(number)], x_out.at[:, chunk(number)], sems.at[10 + number]
            )
        )
        stores[-1].start()
    for store in stores:
        store.wait()


def update_second(cells, xh, xl, yh, yl, gh, gl, before, after, tiles, values):
    return pl.pallas_call(
        update_second_kernel,
        in_specs=[VMEM] + [ANY] * 10,
        out_specs=ANY,
        out_shape=jax.ShapeDtypeStruct((K, CELLS), F32),
        scratch_shapes=[pltpu.VMEM((K, CELLS), F32)]
        + vmem_pair(CELLS, K)
        + vmem_pair(K + PAD, WINDOW)
        + vmem_pair(CELLS, WINDOW)
        + [
            pltpu.VMEM((K, 2 * SLAB), F32),
            pltpu.VMEM((CELLS, WINDOW), F32),
            pltpu.SemaphoreType.DMA((13,)),
        ],
        compiler_params=PARAMS,
        cost_estimate=pl.CostEstimate(
            flops=10 * K * CELLS * WINDOW, bytes_accessed=25 << 20, transcendentals=0
        ),
        name="update_second",
    )(values, cells, xh, xl, yh, yl, gh, gl, before, after, tiles)


def observe_all_kernel(sizes, op_ref, at_ref, values_ref, *refs):
    count = len(sizes)
    pieces, (t_in, ops), refs = refs[:count], refs[count : count + 2], refs[count + 2 :]
    y_out, yh_out, yl_out, all_y, tiles, fresh, xh, xl, yh, yl, gh, gl, oph, opl, sems, more = refs
    pairs = []
    for piece, size in zip(pieces, sizes):
        for q in range(size):
            at = pl.multiple_of(at_ref[len(pairs)] * ROWS, ROWS)
            pairs.append((piece.at[q * ROWS : (q + 1) * ROWS, :], all_y.at[pl.ds(at, ROWS), :]))
    loads = copies(sems, pairs)
    tile_load = pltpu.make_async_copy(t_in, tiles, more.at[0])
    tile_load.start()
    for load in loads:
        load.wait()
    split_cells(all_y, WINDOW, OB, xh, xl)
    tile_load.wait()
    for number in range(WINDOW // CHUNK):
        split_observed(all_y, number, number, values_ref, yh, yl)
        gains(chunk(number), chunk(number), tiles, xh, xl, yh, yl, gh, gl)
    stores = [
        pltpu.make_async_copy(yh, yh_out, more.at[1]),
        pltpu.make_async_copy(yl, yl_out, more.at[2]),
    ]
    for store in stores:
        store.start()
    for number in range(SLAB // CHUNK):
        cells = all_y[:, WINDOW + number * CHUNK : WINDOW + (number + 1) * CHUNK]
        fresh[:, chunk(number)] = cells + increment(number, yh, yl, gh, gl)
    zero = jnp.zeros((BLK, BLK), F32)
    for number in range(SLAB // CHUNK):
        first, second = ops[op_ref[1, 2 * number]], ops[op_ref[1, 2 * number + 1]]
        pair = jnp.concatenate(
            [jnp.concatenate([first, zero], 1), jnp.concatenate([zero, second], 1)], 0
        )
        oph[chunk(number), :], opl[chunk(number), :] = split_high_low(pair)

    @pl.loop(0, K // CHUNK)
    def _(part):
        rows = pl.ds(pl.multiple_of(part * CHUNK, CHUNK), CHUNK)
        for number in range(SLAB // CHUNK):
            high, low = split_high_low(fresh[rows, chunk(number)])
            op_high, op_low = oph[chunk(number), :], opl[chunk(number), :]
            fresh[rows, chunk(number)] = (
                dot_nt(high, op_high) + dot_nt(high, op_low) + dot_nt(low, op_high)
            )

    stores.append(pltpu.make_async_copy(fresh, y_out, more.at[3]))
    stores[-1].start()
    for store in stores:
        store.wait()


def observe_all(pieces, places, tiles, values, op_select, op_table):
    sizes = tuple(piece.shape[0] // ROWS for piece in pieces)
    return pl.pallas_call(
        functools.partial(observe_all_kernel, sizes),
        in_specs=[SMEM, SMEM, VMEM] + [ANY] * (len(pieces) + 1) + [VMEM],
        out_specs=[ANY] * 3,
        out_shape=[jax.ShapeDtypeStruct((K, SLAB), F32)] + bf16_pair(K + PAD, WINDOW),
        scratch_shapes=[
            pltpu.VMEM((K, WINDOW + SLAB), F32),
            pltpu.VMEM((SLAB, WINDOW), F32),
            pltpu.VMEM((K, SLAB), F32),
        ]
        + vmem_pair(SLAB, K)
        + vmem_pair(K + PAD, WINDOW)
        + vmem_pair(SLAB, WINDOW)
        + vmem_pair(SLAB, CHUNK)
        + [pltpu.SemaphoreType.DMA((sum(sizes),)), pltpu.SemaphoreType.DMA((4,))],
        compiler_params=PARAMS,
        cost_estimate=pl.CostEstimate(
            flops=12 * K * SLAB * WINDOW, bytes_accessed=20 << 20, transcendentals=0
        ),
        name="observe_all",
    )(op_select, places, values, *pieces, tiles, op_table)


BOTH = ("member", "space")


def send(value, target):
    pairs = []
    for index in range(128):
        member, slab = index // 4, index % 4
        y_hi, x, z = target(member // 16, member // 4 % 4, member % 4, slab // 2, slab % 2)[:3]
        y_lo, core = target(member // 16, member // 4 % 4, member % 4, slab // 2, slab % 2)[3:]
        pairs.append((index, (y_hi % 2 * 16 + x % 4 * 4 + z % 4) * 4 + y_lo % 2 * 2 + core % 2))
    return lax.ppermute(value, BOTH, pairs)


def along_x(value, step):
    return send(value, lambda h, x, z, y, c: (h, x + step, z, y, c))


def along_z(value, step):
    return send(value, lambda h, x, z, y, c: (h, x, z + step, y, c))


def to_slab(value, step, flip):
    def target(h, x, z, y, c):
        slab = (2 * y + c + step) % 4
        return (h + flip, x, z, slab // 2, slab % 2)

    return send(value, target)


def neighbour_slabs(value):
    def up(h, x, z, y, c):
        if c == 0:
            return (h, x, z, y, 1)
        return (h + y, x, z, 1 - y, 0)

    def down(h, x, z, y, c):
        if c == 1:
            return (h, x, z, y, 0)
        return (h + 1 - y, x, z, 1 - y, 1)

    return send(value, up), send(value, down)


def together(*values):
    return lax.optimization_barrier(values)


def gather_pieces(observed, raw):
    rows = jnp.concatenate([observed, raw], axis=1)
    prev, after = to_slab(observed, 1, 0), to_slab(observed, -1, 0)
    prev_f, after_f = to_slab(observed, 1, 1), to_slab(observed, -1, 1)
    rows_f = to_slab(rows, 0, 1)
    prev, after, prev_f, after_f, rows_f = together(prev, after, prev_f, after_f, rows_f)
    near = jnp.concatenate([prev, observed, after, raw], axis=1)
    far = jnp.concatenate([prev_f, rows_f[:, :SLAB], after_f, rows_f[:, SLAB:]], axis=1)
    near, far = together(near, far)
    parts = together(
        *[along_z(near, d) for d in (1, -1, 2)], *[along_x(far, d) for d in (1, -1, 2)]
    )
    halves = [
        jnp.concatenate([near, parts[0]], axis=0),
        jnp.concatenate([parts[1], parts[2]], axis=0),
        jnp.concatenate([far, parts[3]], axis=0),
        jnp.concatenate([parts[4], parts[5]], axis=0),
    ]
    return together(*halves)


def forwarded_halves(near_a, near_b, far_a, far_b):
    return along_x(near_a, 1), along_x(near_b, -1), along_z(far_a, 1), along_z(far_b, -1)


def other_halves(near_a, near_b, far_a, far_b):
    return along_x(near_b, 1), along_x(near_a, -1), along_z(far_b, 1), along_z(far_a, -1)


def piece_places():
    low, high = (0, -1), (1, 2)
    offsets = [(0, 0, d) for d in low + high] + [(1, d, 0) for d in low + high]
    offsets += [(0, -1, d) for d in low] + [(0, 1, d) for d in high]
    offsets += [(1, d, -1) for d in low] + [(1, d, 1) for d in high]
    offsets += [(0, -1, d) for d in high] + [(0, 1, d) for d in low]
    offsets += [(1, d, -1) for d in high] + [(1, d, 1) for d in low]
    offsets += [(0, 2, d) for d in low + high] + [(1, d, 2) for d in low + high]
    member = lax.axis_index("member")
    flip, dx, dz = (jnp.array(column, jnp.int32) for column in zip(*offsets))
    y_hi, x, z = member // 16, member // 4 % 4, member % 4
    return ((y_hi + flip) % 2 * 16 + (x + dx + 4) % 4 * 4 + (z + dz + 4) % 4).astype(jnp.int32)


def window_rows(rows):
    count = lax.axis_size("space")
    slab = lax.axis_index("space")
    by_slab = rows.reshape(BATCHES, count, OB * BLK)
    pick = (slab - 1 + jnp.arange(3, dtype=jnp.int32)) % count
    return by_slab[:, pick].reshape(BATCHES, WIN * BLK)


def per_device(
    states, obs_values, obs_weights, obs_cell, op_select, op_table, loc_obs, loc_tile, loc_tiles
):
    obs_cell, op_select = obs_cell[:, 0], op_select[:, 0]
    loc_obs, loc_tile = loc_obs[:, 0], loc_tile[:, 0]
    values, weights = window_rows(obs_values), window_rows(obs_weights)

    observed, raw = observe_members(states, obs_cell, op_select, op_table)
    halves = gather_pieces(observed, raw)

    loc = jnp.concatenate([loc_obs[0], loc_tile[0]], axis=1)
    loc = jnp.pad(loc, ((0, 8 - CB_DEV), (0, BLK - 2 * LOC)))
    loc = jnp.broadcast_to(loc[None], (MEMBERS, 8, BLK))
    *halves, loc, states = together(*halves, loc, states)
    first = forwarded_halves(*halves)
    loc = lax.all_to_all(loc, "member", 0, 0, tiled=True)
    loc = loc[:, :CB_DEV, : 2 * LOC].reshape(MEMBERS * CB_DEV, 2 * LOC)[obs_cell[1]]
    *first, loc, states = together(*first, loc, states)
    second = other_halves(*halves)
    third = (
        along_x(first[0], 1),
        along_x(first[1], -1),
        along_z(first[2], 1),
        along_z(first[3], -1),
    )
    tiles_obs = weighted_tiles(loc[:, :LOC], loc[:, LOC:], loc_tiles, weights)
    tiles = weighted_tiles(
        jnp.concatenate([loc_obs[0], loc_obs[1]], axis=0),
        jnp.concatenate([loc_tile[0], loc_tile[1]], axis=0),
        loc_tiles,
        weights,
    )
    cells = lax.all_to_all(states, "member", split_axis=1, concat_axis=0, tiled=True)
    *pieces, tiles, tiles_obs = together(*halves, *first, *second, *third, tiles, tiles_obs)

    observed, yh, yl = observe_all(
        pieces, piece_places(), tiles_obs, values[:1], op_select, op_table
    )
    before, after = neighbour_slabs(observed)
    parts = update_first(cells, yh, yl, observed, tiles, values[1:])
    cells = update_second(*parts, before, after, tiles, values[1:])
    return lax.all_to_all(cells, "member", split_axis=0, concat_axis=1, tiled=True)


def solution(mesh):
    placed = (
        P("member", "space"),
        P(),
        P(),
        P(None, "space", None),
        P(None, "space", None),
        P(),
        P(None, "space", "member", None),
        P(None, "space", "member", None),
        P(),
    )
    return jax.shard_map(
        per_device, mesh=mesh, in_specs=placed, out_specs=P("member", "space"), check_vma=False
    )
```

```python
import functools

import jax
import jax.numpy as jnp
from jax import lax
from jax.experimental import pallas as pl
from jax.experimental.pallas import tpu as pltpu
from jax.sharding import PartitionSpec as P

K = 1024
BLK = 128
OB = 4
LOC = 8
BATCHES = 2
MEMBERS = 32
CB_DEV = 6
WIN = 3 * OB
PAD = 16
VMEM_BYTES = 60 * 1024 * 1024

F32 = jnp.float32
BF16 = jnp.bfloat16
PARAMS = pltpu.CompilerParams(vmem_limit_bytes=VMEM_BYTES)


def split_high_low(value):
    high = value.astype(BF16)
    low = (value - high.astype(F32)).astype(BF16)
    return high, low


def dot_nn(a, b):
    return lax.dot_general(a, b, (((1,), (0,)), ((), ())), preferred_element_type=F32)


def dot_nt(a, b, precision=None):
    return lax.dot_general(
        a, b, (((1,), (1,)), ((), ())), preferred_element_type=F32, precision=precision
    )


def observe_kernel(cell_ref, op_ref, *refs):
    first, second, ops = refs[:OB], refs[OB : 2 * OB], refs[2 * OB : 3 * OB]
    loc_ref, out_ref = refs[3 * OB :]
    out_ref[:, 2 * OB * BLK :] = loc_ref[...]
    for o in range(OB):
        out_ref[:, o * BLK : (o + 1) * BLK] = dot_nt(
            first[o][...], ops[o][0], lax.Precision.HIGHEST
        )
        out_ref[:, (OB + o) * BLK : (OB + o + 1) * BLK] = second[o][...]


def observe_members(states, obs_cell, op_select, op_table, loc):
    members = states.shape[0]

    def cells_of(batch, o):
        return pl.BlockSpec((members, BLK), lambda i, cell, op: (0, cell[batch, o]))

    def operator_of(o):
        return pl.BlockSpec((1, BLK, BLK), lambda i, cell, op: (op[0, o], 0, 0))

    width = (2 * OB + 1) * BLK
    whole = pl.BlockSpec((members, width), lambda i, cell, op: (0, 0))
    shape = jax.ShapeDtypeStruct((members, width), F32)
    return pl.pallas_call(
        observe_kernel,
        grid_spec=pltpu.PrefetchScalarGridSpec(
            num_scalar_prefetch=2,
            grid=(1,),
            in_specs=[cells_of(b, o) for b in range(BATCHES) for o in range(OB)]
            + [operator_of(o) for o in range(OB)]
            + [pl.BlockSpec((members, BLK), lambda i, cell, op: (0, 0))],
            out_specs=whole,
        ),
        out_shape=shape,
        compiler_params=PARAMS,
        name="observe",
    )(obs_cell, op_select, *([states] * (2 * OB)), *([op_table] * OB), loc)


def tiles_kernel(obs_ref, tile_ref, tiles_ref, weights_ref, out_ref):
    n = pl.program_id(0)
    out_ref[...] = jnp.zeros_like(out_ref)
    for l in range(LOC):
        cols = pl.ds(pl.multiple_of(obs_ref[n, l] * BLK, BLK), BLK)
        scale = weights_ref[0, :, cols] * (-0.5 / (K - 1))
        out_ref[:, cols] += tiles_ref[tile_ref[n, l]] * scale


def weighted_tiles(loc_obs, loc_tile, loc_tiles, weights):
    blocks = loc_obs.shape[0]
    return pl.pallas_call(
        tiles_kernel,
        grid_spec=pltpu.PrefetchScalarGridSpec(
            num_scalar_prefetch=2,
            grid=(blocks,),
            in_specs=[
                pl.BlockSpec(loc_tiles.shape, lambda n, a, b: (0, 0, 0)),
                pl.BlockSpec(
                    (1, 1, WIN * BLK),
                    lambda n, a, b: (jnp.where((n >= CB_DEV) & (n < 2 * CB_DEV), 1, 0), 0, 0),
                ),
            ],
            out_specs=pl.BlockSpec((BLK, WIN * BLK), lambda n, a, b: (n, 0)),
        ),
        out_shape=jax.ShapeDtypeStruct((blocks * BLK, WIN * BLK), F32),
        compiler_params=PARAMS,
        cost_estimate=pl.CostEstimate(flops=1 << 22, bytes_accessed=14 << 20, transcendentals=0),
        name="weighted_tiles",
    )(loc_obs, loc_tile, loc_tiles, weights.reshape(BATCHES, 1, WIN * BLK))


CHUNK = 2 * BLK
SLAB = OB * BLK
ROWS = 32
ANY = pl.BlockSpec(memory_space=pl.ANY)
SMEM = pl.BlockSpec(memory_space=pltpu.SMEM)
VMEM = pl.BlockSpec(memory_space=pltpu.VMEM)


def chunk(number):
    return slice(number * CHUNK, (number + 1) * CHUNK)


def split_observed(y_ref, src, dst, values_ref, yh, yl):
    y = y_ref[:, chunk(src)]
    mean = jnp.sum(y, axis=0, keepdims=True) * (1.0 / K)
    yh[0:K, chunk(dst)], yl[0:K, chunk(dst)] = split_high_low(y - mean)
    shift = jnp.broadcast_to(-2.0 * (values_ref[:, chunk(dst)] - mean), (PAD, CHUNK))
    yh[K : K + PAD, chunk(dst)], yl[K : K + PAD, chunk(dst)] = split_high_low(shift)


def split_cells(x_ref, col0, nb, xh, xl):
    for n in range(nb):
        x = x_ref[:, col0 + n * BLK : col0 + (n + 1) * BLK]
        anom = x - jnp.sum(x, axis=0, keepdims=True) * (1.0 / K)
        rows = slice(n * BLK, (n + 1) * BLK)
        xh[rows, :], xl[rows, :] = split_high_low(anom.T)


def gains(cols, tile_cols, tiles_ref, xh, xl, yh, yl, gh, gl):
    high, low = yh[0:K, cols], yl[0:K, cols]
    cov = dot_nn(xh[...], high) + dot_nn(xh[...], low) + dot_nn(xl[...], high)
    gh[:, cols], gl[:, cols] = split_high_low(cov * tiles_ref[:, tile_cols])


def increment(number, yh, yl, gh, gl):
    high, low = gh[chunk(number), :], gl[chunk(number), :]
    inc = dot_nt(yh[...], high) + dot_nt(yh[...], low) + dot_nt(yl[...], high)
    return inc[0:K] + inc[K : K + 1]


def bf16_pair(rows, cols):
    return [jax.ShapeDtypeStruct((rows, cols), BF16)] * 2


def vmem_pair(rows, cols):
    return [pltpu.VMEM((rows, cols), BF16)] * 2


def copies(sems, pairs):
    out = [pltpu.make_async_copy(src, dst, sems.at[i]) for i, (src, dst) in enumerate(pairs)]
    for copy in out:
        copy.start()
    return out


CELLS = CB_DEV * BLK
WINDOW = WIN * BLK
OWN = slice(SLAB, 2 * SLAB)


def own_gains_kernel(
    row0, values_ref, x_in, own_in, t_in,
    xh_out, xl_out, yh_out, yl_out, gh_out, gl_out,
    x, own, tiles, xh, xl, yh, yl, gh, gl, sems,
):
    cells = x.shape[1]
    x_load, own_load, t_load = copies(
        sems, [(x_in, x), (own_in, own), (t_in.at[row0 : row0 + cells, OWN], tiles)]
    )
    x_load.wait()
    split_cells(x, 0, cells // BLK, xh, xl)
    stores = []

    def store(source, target):
        stores.append(pltpu.make_async_copy(source, target, sems.at[3 + len(stores)]))
        stores[-1].start()

    store(xh, xh_out)
    store(xl, xl_out)
    own_load.wait()
    t_load.wait()
    for number in range(SLAB // CHUNK):
        split_observed(own, number, number, values_ref, yh, yl)
        gains(chunk(number), chunk(number), tiles, xh, xl, yh, yl, gh, gl)
    store(yh, yh_out)
    store(yl, yl_out)
    store(gh, gh_out)
    store(gl, gl_out)
    for copy in stores:
        copy.wait()


def own_gains(cells, own, tiles, row0, values, name):
    count = cells.shape[1]
    return pl.pallas_call(
        functools.partial(own_gains_kernel, row0),
        in_specs=[VMEM] + [ANY] * 3,
        out_specs=[ANY] * 6,
        out_shape=bf16_pair(count, K) + bf16_pair(K + PAD, SLAB) + bf16_pair(count, SLAB),
        scratch_shapes=[
            pltpu.VMEM((K, count), F32),
            pltpu.VMEM((K, SLAB), F32),
            pltpu.VMEM((count, SLAB), F32),
        ]
        + vmem_pair(count, K)
        + vmem_pair(K + PAD, SLAB)
        + vmem_pair(count, SLAB)
        + [pltpu.SemaphoreType.DMA((9,))],
        compiler_params=PARAMS,
        cost_estimate=pl.CostEstimate(
            flops=6 * K * count * SLAB, bytes_accessed=14 << 20, transcendentals=0
        ),
        name=name,
    )(values[:, OWN], cells, own, tiles)


def update_kernel(
    row0, observing, values_ref,
    x_in, xh_in, xl_in, yh_in, yl_in, gh_in, gl_in, before_in, after_in, t_in, *refs,
):
    if observing:
        op_ref, ops, x_out, oph, opl, *refs = refs
    else:
        x_out, *refs = refs
    x, xh, xl, yh, yl, gh, gl, y, tiles, sems = refs
    cells = x.shape[1]
    loads = copies(
        sems,
        [
            (before_in, y.at[:, 0:SLAB]),
            (xh_in, xh),
            (xl_in, xl),
            (t_in.at[row0 : row0 + cells, :], tiles),
            (after_in, y.at[:, SLAB : 2 * SLAB]),
            (yh_in, yh.at[:, OWN]),
            (yl_in, yl.at[:, OWN]),
            (gh_in, gh.at[:, OWN]),
            (gl_in, gl.at[:, OWN]),
            (x_in, x),
        ],
    )
    count = len(loads)
    per = SLAB // CHUNK
    for load in loads[:4]:
        load.wait()
    for number in range(per):
        split_observed(y, number, number, values_ref, yh, yl)
        gains(chunk(number), chunk(number), tiles, xh, xl, yh, yl, gh, gl)
    loads[4].wait()
    for number in range(per):
        split_observed(y, per + number, 2 * per + number, values_ref, yh, yl)
        cols = chunk(2 * per + number)
        gains(cols, cols, tiles, xh, xl, yh, yl, gh, gl)
    for load in loads[5:]:
        load.wait()
    stores = []

    def store(source, target):
        stores.append(pltpu.make_async_copy(source, target, sems.at[count + len(stores)]))
        stores[-1].start()

    for number in range(cells // CHUNK):
        x[:, chunk(number)] += increment(number, yh, yl, gh, gl)
        if not observing:
            store(x.at[:, chunk(number)], x_out.at[:, chunk(number)])
    if observing:
        zero = jnp.zeros((BLK, BLK), F32)
        for number in range(cells // CHUNK):
            first, second = ops[op_ref[1, 2 * number]], ops[op_ref[1, 2 * number + 1]]
            pair = jnp.concatenate(
                [jnp.concatenate([first, zero], 1), jnp.concatenate([zero, second], 1)], 0
            )
            oph[chunk(number), :], opl[chunk(number), :] = split_high_low(pair)

        @pl.loop(0, K // CHUNK)
        def _(part):
            rows = pl.ds(pl.multiple_of(part * CHUNK, CHUNK), CHUNK)
            for number in range(cells // CHUNK):
                high, low = split_high_low(x[rows, chunk(number)])
                op_high, op_low = oph[chunk(number), :], opl[chunk(number), :]
                x[rows, chunk(number)] = (
                    dot_nt(high, op_high) + dot_nt(high, op_low) + dot_nt(low, op_high)
                )

        store(x, x_out)
    for copy in stores:
        copy.wait()


def update(cells, split, before, after, tiles, row0, values, name, operators=None):
    count = cells.shape[1]
    observing = operators is not None
    return pl.pallas_call(
        functools.partial(update_kernel, row0, observing),
        in_specs=[VMEM] + [ANY] * 10 + ([SMEM, VMEM] if observing else []),
        out_specs=ANY,
        out_shape=jax.ShapeDtypeStruct((K, count), F32),
        scratch_shapes=(vmem_pair(count, CHUNK) if observing else [])
        + [pltpu.VMEM((K, count), F32)]
        + vmem_pair(count, K)
        + vmem_pair(K + PAD, WINDOW)
        + vmem_pair(count, WINDOW)
        + [
            pltpu.VMEM((K, 2 * SLAB), F32),
            pltpu.VMEM((count, WINDOW), F32),
            pltpu.SemaphoreType.DMA((13,)),
        ],
        compiler_params=PARAMS,
        cost_estimate=pl.CostEstimate(
            flops=10 * K * count * WINDOW, bytes_accessed=25 << 20, transcendentals=0
        ),
        name=name,
    )(values, cells, *split, before, after, tiles, *(operators or ()))


def assemble_kernel(sizes, at_ref, *refs):
    count = len(sizes)
    pieces, (observed, raw, loc, sems) = refs[:count], refs[count:]
    pairs, place = [], 0
    for piece, size in zip(pieces, sizes):
        for q in range(size):
            rows = pl.ds(pl.multiple_of(at_ref[place] * ROWS, ROWS), ROWS)
            part = piece.at[q * ROWS : (q + 1) * ROWS, :]
            pairs.append((part.at[:, 0:SLAB], observed.at[rows, :]))
            pairs.append((part.at[:, SLAB : 2 * SLAB], raw.at[rows, :]))
            rows = pl.ds(pl.multiple_of(at_ref[place] * 8, 8), 8)
            part = piece.at[q * ROWS : q * ROWS + 8, 2 * SLAB : 2 * SLAB + BLK]
            pairs.append((part, loc.at[rows, :]))
            place += 1
    for copy in copies(sems, pairs):
        copy.wait()


def assemble(pieces, places):
    sizes = tuple(piece.shape[0] // ROWS for piece in pieces)
    return pl.pallas_call(
        functools.partial(assemble_kernel, sizes),
        in_specs=[SMEM] + [ANY] * len(pieces),
        out_specs=[ANY] * 3,
        out_shape=[jax.ShapeDtypeStruct((K, SLAB), F32)] * 2
        + [jax.ShapeDtypeStruct((8 * MEMBERS, BLK), F32)],
        scratch_shapes=[pltpu.SemaphoreType.DMA((3 * sum(sizes),))],
        compiler_params=PARAMS,
        cost_estimate=pl.CostEstimate(flops=0, bytes_accessed=8 << 20, transcendentals=0),
        name="assemble",
    )(places, *pieces)


BOTH = ("member", "space")


def send(value, target):
    pairs = []
    for index in range(128):
        member, slab = index // 4, index % 4
        y_hi, x, z = target(member // 16, member // 4 % 4, member % 4, slab // 2, slab % 2)[:3]
        y_lo, core = target(member // 16, member // 4 % 4, member % 4, slab // 2, slab % 2)[3:]
        pairs.append((index, (y_hi % 2 * 16 + x % 4 * 4 + z % 4) * 4 + y_lo % 2 * 2 + core % 2))
    return lax.ppermute(value, BOTH, pairs)


def along_x(value, step):
    return send(value, lambda h, x, z, y, c: (h, x + step, z, y, c))


def along_z(value, step):
    return send(value, lambda h, x, z, y, c: (h, x, z + step, y, c))


def neighbour_slabs(value):
    def up(h, x, z, y, c):
        if c == 0:
            return (h, x, z, y, 1)
        return (h + y, x, z, 1 - y, 0)

    def down(h, x, z, y, c):
        if c == 1:
            return (h, x, z, y, 0)
        return (h + 1 - y, x, z, 1 - y, 1)

    return send(value, up), send(value, down)


def together(*values):
    return lax.optimization_barrier(values)


STEPS = (1, -1, 2)


def piece_places():
    ring = (0, -1, 1, 2)
    offsets = [(0, 0, d) for d in ring] + [(1, d, 0) for d in ring]
    offsets += [(0, s, d) for s in ring[1:] for d in ring]
    offsets += [(1, d, s) for s in ring[1:] for d in ring]
    member = lax.axis_index("member")
    flip, dx, dz = (jnp.array(column, jnp.int32) for column in zip(*offsets))
    y_hi, x, z = member // 16, member // 4 % 4, member % 4
    return ((y_hi + flip) % 2 * 16 + (x + dx + 4) % 4 * 4 + (z + dz + 4) % 4).astype(jnp.int32)


def window_rows(rows):
    count = lax.axis_size("space")
    slab = lax.axis_index("space")
    by_slab = rows.reshape(BATCHES, count, OB * BLK)
    pick = (slab - 1 + jnp.arange(3, dtype=jnp.int32)) % count
    return by_slab[:, pick].reshape(BATCHES, WIN * BLK)


def per_device(
    states, obs_values, obs_weights, obs_cell, op_select, op_table, loc_obs, loc_tile, loc_tiles
):
    obs_cell, op_select = obs_cell[:, 0], op_select[:, 0]
    loc_obs, loc_tile = loc_obs[:, 0], loc_tile[:, 0]
    values, weights = window_rows(obs_values), window_rows(obs_weights)

    loc = jnp.concatenate([loc_obs[0], loc_tile[0]], axis=1).astype(F32)
    loc = jnp.pad(loc, ((0, ROWS - CB_DEV), (0, BLK - 2 * LOC)))
    near = observe_members(states, obs_cell, op_select, op_table, loc)
    far = send(near, lambda h, x, z, y, c: (1 - h, x, z, y, c))
    near, far = together(near, far)
    parts = together(*[along_z(near, d) for d in STEPS], *[along_x(far, d) for d in STEPS])
    near = jnp.concatenate([near, *parts[:3]], axis=0)
    far = jnp.concatenate([far, *parts[3:]], axis=0)
    near, far = together(near, far)
    pieces = [near, far, *[along_x(near, d) for d in STEPS], *[along_z(far, d) for d in STEPS]]
    tiles = weighted_tiles(
        jnp.concatenate([loc_obs[0], loc_obs[1]], axis=0),
        jnp.concatenate([loc_tile[0], loc_tile[1]], axis=0),
        loc_tiles,
        weights,
    )
    cells = lax.all_to_all(states, "member", split_axis=1, concat_axis=0, tiled=True)
    *pieces, tiles, cells = together(*pieces, tiles, cells)

    observed, raw, loc = assemble(pieces, piece_places())
    loc = loc.reshape(MEMBERS, 8, BLK)[:, :CB_DEV, : 2 * LOC].reshape(MEMBERS * CB_DEV, 2 * LOC)
    loc = loc[obs_cell[1]].astype(jnp.int32)
    before, after = neighbour_slabs(observed)
    tiles_obs = weighted_tiles(loc[:, :LOC], loc[:, LOC:], loc_tiles, weights)
    split_raw = own_gains(raw, observed, tiles_obs, 0, values[:1], "own_gains_observed")
    split = own_gains(cells, observed, tiles, 0, values[:1], "own_gains_first")
    *split, before, after = together(*split, before, after)
    observed = update(
        raw, split_raw, before, after, tiles_obs, 0, values[:1], "update_observed",
        (op_select, op_table),
    )
    before_next, after_next = neighbour_slabs(observed)
    cells = update(cells, split, before, after, tiles, 0, values[:1], "update_first")
    split = own_gains(cells, observed, tiles, CELLS, values[1:], "own_gains_second")
    cells = update(
        cells, split, before_next, after_next, tiles, CELLS, values[1:], "update_second"
    )
    return lax.all_to_all(cells, "member", split_axis=0, concat_axis=1, tiled=True)


def solution(mesh):
    placed = (
        P("member", "space"),
        P(),
        P(),
        P(None, "space", None),
        P(None, "space", None),
        P(),
        P(None, "space", "member", None),
        P(None, "space", "member", None),
        P(),
    )
    return jax.shard_map(
        per_device, mesh=mesh, in_specs=placed, out_specs=P("member", "space"), check_vma=False
    )
```

```python
import functools

import jax
import jax.numpy as jnp
from jax import lax
from jax.experimental import pallas as pl
from jax.experimental.pallas import tpu as pltpu
from jax.sharding import PartitionSpec as P

K = 1024
BLK = 128
OB = 4
LOC = 8
BATCHES = 2
MEMBERS = 32
CB_DEV = 6
WIN = 3 * OB
PAD = 16
VMEM_BYTES = 60 * 1024 * 1024

F32 = jnp.float32
BF16 = jnp.bfloat16
PARAMS = pltpu.CompilerParams(vmem_limit_bytes=VMEM_BYTES)


def split_high_low(value):
    high = value.astype(BF16)
    low = (value - high.astype(F32)).astype(BF16)
    return high, low


def dot_nn(a, b):
    return lax.dot_general(a, b, (((1,), (0,)), ((), ())), preferred_element_type=F32)


def dot_nt(a, b, precision=None):
    return lax.dot_general(
        a, b, (((1,), (1,)), ((), ())), preferred_element_type=F32, precision=precision
    )


def observe_kernel(cell_ref, op_ref, *refs):
    first, second, ops = refs[:OB], refs[OB : 2 * OB], refs[2 * OB : 3 * OB]
    loc_ref, out_ref = refs[3 * OB :]
    out_ref[:, 2 * OB * BLK :] = loc_ref[...]
    for o in range(OB):
        out_ref[:, o * BLK : (o + 1) * BLK] = dot_nt(
            first[o][...], ops[o][0], lax.Precision.HIGHEST
        )
        out_ref[:, (OB + o) * BLK : (OB + o + 1) * BLK] = second[o][...]


def observe_members(states, obs_cell, op_select, op_table, loc):
    members = states.shape[0]

    def cells_of(batch, o):
        return pl.BlockSpec((members, BLK), lambda i, cell, op: (0, cell[batch, o]))

    def operator_of(o):
        return pl.BlockSpec((1, BLK, BLK), lambda i, cell, op: (op[0, o], 0, 0))

    width = (2 * OB + 1) * BLK
    whole = pl.BlockSpec((members, width), lambda i, cell, op: (0, 0))
    shape = jax.ShapeDtypeStruct((members, width), F32)
    return pl.pallas_call(
        observe_kernel,
        grid_spec=pltpu.PrefetchScalarGridSpec(
            num_scalar_prefetch=2,
            grid=(1,),
            in_specs=[cells_of(b, o) for b in range(BATCHES) for o in range(OB)]
            + [operator_of(o) for o in range(OB)]
            + [pl.BlockSpec((members, BLK), lambda i, cell, op: (0, 0))],
            out_specs=whole,
        ),
        out_shape=shape,
        compiler_params=PARAMS,
        name="observe",
    )(obs_cell, op_select, *([states] * (2 * OB)), *([op_table] * OB), loc)


def tiles_kernel(obs_ref, tile_ref, tiles_ref, weights_ref, out_ref):
    n = pl.program_id(0)
    out_ref[...] = jnp.zeros_like(out_ref)
    for l in range(LOC):
        cols = pl.ds(pl.multiple_of(obs_ref[n, l] * BLK, BLK), BLK)
        scale = weights_ref[0, :, cols] * (-0.5 / (K - 1))
        out_ref[:, cols] += tiles_ref[tile_ref[n, l]] * scale


def weighted_tiles(loc_obs, loc_tile, loc_tiles, weights):
    blocks = loc_obs.shape[0]
    return pl.pallas_call(
        tiles_kernel,
        grid_spec=pltpu.PrefetchScalarGridSpec(
            num_scalar_prefetch=2,
            grid=(blocks,),
            in_specs=[
                pl.BlockSpec(loc_tiles.shape, lambda n, a, b: (0, 0, 0)),
                pl.BlockSpec(
                    (1, 1, WIN * BLK),
                    lambda n, a, b: (jnp.where((n >= CB_DEV) & (n < 2 * CB_DEV), 1, 0), 0, 0),
                ),
            ],
            out_specs=pl.BlockSpec((BLK, WIN * BLK), lambda n, a, b: (n, 0)),
        ),
        out_shape=jax.ShapeDtypeStruct((blocks * BLK, WIN * BLK), F32),
        compiler_params=PARAMS,
        cost_estimate=pl.CostEstimate(flops=1 << 22, bytes_accessed=14 << 20, transcendentals=0),
        name="weighted_tiles",
    )(loc_obs, loc_tile, loc_tiles, weights.reshape(BATCHES, 1, WIN * BLK))


CHUNK = 2 * BLK
SLAB = OB * BLK
ROWS = 32
ANY = pl.BlockSpec(memory_space=pl.ANY)
SMEM = pl.BlockSpec(memory_space=pltpu.SMEM)
VMEM = pl.BlockSpec(memory_space=pltpu.VMEM)


def chunk(number):
    return slice(number * CHUNK, (number + 1) * CHUNK)


def split_observed(y_ref, src, dst, values_ref, yh, yl):
    y = y_ref[:, chunk(src)]
    mean = jnp.sum(y, axis=0, keepdims=True) * (1.0 / K)
    yh[0:K, chunk(dst)], yl[0:K, chunk(dst)] = split_high_low(y - mean)
    shift = jnp.broadcast_to(-2.0 * (values_ref[:, chunk(dst)] - mean), (PAD, CHUNK))
    yh[K : K + PAD, chunk(dst)], yl[K : K + PAD, chunk(dst)] = split_high_low(shift)


def split_cells(x_ref, col0, nb, xh, xl):
    for n in range(nb):
        x = x_ref[:, col0 + n * BLK : col0 + (n + 1) * BLK]
        anom = x - jnp.sum(x, axis=0, keepdims=True) * (1.0 / K)
        rows = slice(n * BLK, (n + 1) * BLK)
        xh[rows, :], xl[rows, :] = split_high_low(anom.T)


def gains(cols, tile_cols, tiles_ref, xh, xl, yh, yl, gh, gl):
    high, low = yh[0:K, cols], yl[0:K, cols]
    cov = dot_nn(xh[...], high) + dot_nn(xh[...], low) + dot_nn(xl[...], high)
    gh[:, cols], gl[:, cols] = split_high_low(cov * tiles_ref[:, tile_cols])


def increment(number, yh, yl, gh, gl):
    high, low = gh[chunk(number), :], gl[chunk(number), :]
    inc = dot_nt(yh[...], high) + dot_nt(yh[...], low) + dot_nt(yl[...], high)
    return inc[0:K] + inc[K : K + 1]


def bf16_pair(rows, cols):
    return [jax.ShapeDtypeStruct((rows, cols), BF16)] * 2


def vmem_pair(rows, cols):
    return [pltpu.VMEM((rows, cols), BF16)] * 2


def copies(sems, pairs):
    out = [pltpu.make_async_copy(src, dst, sems.at[i]) for i, (src, dst) in enumerate(pairs)]
    for copy in out:
        copy.start()
    return out


CELLS = CB_DEV * BLK
WINDOW = WIN * BLK
OWN = slice(SLAB, 2 * SLAB)


def own_gains_kernel(
    row0, values_ref, x_in, own_in, t_in,
    xh_out, xl_out, yh_out, yl_out, gh_out, gl_out,
    x, own, tiles, xh, xl, yh, yl, gh, gl, sems,
):
    cells = x.shape[1]
    x_load, own_load, t_load = copies(
        sems, [(x_in, x), (own_in, own), (t_in.at[row0 : row0 + cells, OWN], tiles)]
    )
    x_load.wait()
    split_cells(x, 0, cells // BLK, xh, xl)
    stores = []

    def store(source, target):
        stores.append(pltpu.make_async_copy(source, target, sems.at[3 + len(stores)]))
        stores[-1].start()

    store(xh, xh_out)
    store(xl, xl_out)
    own_load.wait()
    t_load.wait()
    for number in range(SLAB // CHUNK):
        split_observed(own, number, number, values_ref, yh, yl)
        gains(chunk(number), chunk(number), tiles, xh, xl, yh, yl, gh, gl)
    store(yh, yh_out)
    store(yl, yl_out)
    store(gh, gh_out)
    store(gl, gl_out)
    for copy in stores:
        copy.wait()


def own_gains(cells, own, tiles, row0, values, name):
    count = cells.shape[1]
    return pl.pallas_call(
        functools.partial(own_gains_kernel, row0),
        in_specs=[VMEM] + [ANY] * 3,
        out_specs=[ANY] * 6,
        out_shape=bf16_pair(count, K) + bf16_pair(K + PAD, SLAB) + bf16_pair(count, SLAB),
        scratch_shapes=[
            pltpu.VMEM((K, count), F32),
            pltpu.VMEM((K, SLAB), F32),
            pltpu.VMEM((count, SLAB), F32),
        ]
        + vmem_pair(count, K)
        + vmem_pair(K + PAD, SLAB)
        + vmem_pair(count, SLAB)
        + [pltpu.SemaphoreType.DMA((9,))],
        compiler_params=PARAMS,
        cost_estimate=pl.CostEstimate(
            flops=6 * K * count * SLAB, bytes_accessed=14 << 20, transcendentals=0
        ),
        name=name,
    )(values[:, OWN], cells, own, tiles)


def update_kernel(
    row0, observing, values_ref,
    x_in, xh_in, xl_in, yh_in, yl_in, gh_in, gl_in, before_in, after_in, t_in, *refs,
):
    if observing:
        op_ref, ops, x_out, oph, opl, *refs = refs
    else:
        x_out, *refs = refs
    x, xh, xl, yh, yl, gh, gl, y, tiles, sems = refs
    cells = x.shape[1]
    loads = copies(
        sems,
        [
            (before_in, y.at[:, 0:SLAB]),
            (xh_in, xh),
            (xl_in, xl),
            (t_in.at[row0 : row0 + cells, :], tiles),
            (after_in, y.at[:, SLAB : 2 * SLAB]),
            (yh_in, yh.at[:, OWN]),
            (yl_in, yl.at[:, OWN]),
            (gh_in, gh.at[:, OWN]),
            (gl_in, gl.at[:, OWN]),
            (x_in, x),
        ],
    )
    count = len(loads)
    per = SLAB // CHUNK
    for load in loads[:4]:
        load.wait()
    for number in range(per):
        split_observed(y, number, number, values_ref, yh, yl)
        gains(chunk(number), chunk(number), tiles, xh, xl, yh, yl, gh, gl)
    loads[4].wait()
    for number in range(per):
        split_observed(y, per + number, 2 * per + number, values_ref, yh, yl)
        cols = chunk(2 * per + number)
        gains(cols, cols, tiles, xh, xl, yh, yl, gh, gl)
    for load in loads[5:]:
        load.wait()
    stores = []

    def store(source, target):
        stores.append(pltpu.make_async_copy(source, target, sems.at[count + len(stores)]))
        stores[-1].start()

    for number in range(cells // CHUNK):
        x[:, chunk(number)] += increment(number, yh, yl, gh, gl)
        if not observing:
            store(x.at[:, chunk(number)], x_out.at[:, chunk(number)])
    if observing:
        zero = jnp.zeros((BLK, BLK), F32)
        for number in range(cells // CHUNK):
            first, second = ops[op_ref[1, 2 * number]], ops[op_ref[1, 2 * number + 1]]
            pair = jnp.concatenate(
                [jnp.concatenate([first, zero], 1), jnp.concatenate([zero, second], 1)], 0
            )
            oph[chunk(number), :], opl[chunk(number), :] = split_high_low(pair)

        @pl.loop(0, K // CHUNK)
        def _(part):
            rows = pl.ds(pl.multiple_of(part * CHUNK, CHUNK), CHUNK)
            for number in range(cells // CHUNK):
                high, low = split_high_low(x[rows, chunk(number)])
                op_high, op_low = oph[chunk(number), :], opl[chunk(number), :]
                x[rows, chunk(number)] = (
                    dot_nt(high, op_high) + dot_nt(high, op_low) + dot_nt(low, op_high)
                )

        store(x, x_out)
    for copy in stores:
        copy.wait()


def update(cells, split, before, after, tiles, row0, values, name, operators=None):
    count = cells.shape[1]
    observing = operators is not None
    return pl.pallas_call(
        functools.partial(update_kernel, row0, observing),
        in_specs=[VMEM] + [ANY] * 10 + ([SMEM, VMEM] if observing else []),
        out_specs=ANY,
        out_shape=jax.ShapeDtypeStruct((K, count), F32),
        scratch_shapes=(vmem_pair(count, CHUNK) if observing else [])
        + [pltpu.VMEM((K, count), F32)]
        + vmem_pair(count, K)
        + vmem_pair(K + PAD, WINDOW)
        + vmem_pair(count, WINDOW)
        + [
            pltpu.VMEM((K, 2 * SLAB), F32),
            pltpu.VMEM((count, WINDOW), F32),
            pltpu.SemaphoreType.DMA((13,)),
        ],
        compiler_params=PARAMS,
        cost_estimate=pl.CostEstimate(
            flops=10 * K * count * WINDOW, bytes_accessed=25 << 20, transcendentals=0
        ),
        name=name,
    )(values, cells, *split, before, after, tiles, *(operators or ()))


def assemble_kernel(sizes, at_ref, *refs):
    count = len(sizes)
    pieces, (observed, raw, loc) = refs[:count], refs[count:]
    place = 0
    for piece, size in zip(pieces, sizes):
        for q in range(size):
            part = slice(q * ROWS, (q + 1) * ROWS)
            rows = pl.ds(pl.multiple_of(at_ref[place] * ROWS, ROWS), ROWS)
            observed[rows, :] = piece[part, 0:SLAB]
            raw[rows, :] = piece[part, SLAB : 2 * SLAB]
            rows = pl.ds(pl.multiple_of(at_ref[place] * 8, 8), 8)
            loc[rows, :] = piece[q * ROWS : q * ROWS + 8, 2 * SLAB : 2 * SLAB + BLK]
            place += 1


def assemble(pieces, places):
    sizes = tuple(piece.shape[0] // ROWS for piece in pieces)
    return pl.pallas_call(
        functools.partial(assemble_kernel, sizes),
        in_specs=[SMEM] + [VMEM] * len(pieces),
        out_specs=[VMEM] * 3,
        out_shape=[jax.ShapeDtypeStruct((K, SLAB), F32)] * 2
        + [jax.ShapeDtypeStruct((8 * MEMBERS, BLK), F32)],
        compiler_params=PARAMS,
        cost_estimate=pl.CostEstimate(flops=0, bytes_accessed=8 << 20, transcendentals=0),
        name="assemble",
    )(places, *pieces)


BOTH = ("member", "space")


def send(value, target):
    pairs = []
    for index in range(128):
        member, slab = index // 4, index % 4
        y_hi, x, z = target(member // 16, member // 4 % 4, member % 4, slab // 2, slab % 2)[:3]
        y_lo, core = target(member // 16, member // 4 % 4, member % 4, slab // 2, slab % 2)[3:]
        pairs.append((index, (y_hi % 2 * 16 + x % 4 * 4 + z % 4) * 4 + y_lo % 2 * 2 + core % 2))
    return lax.ppermute(value, BOTH, pairs)


def along_x(value, step):
    return send(value, lambda h, x, z, y, c: (h, x + step, z, y, c))


def along_z(value, step):
    return send(value, lambda h, x, z, y, c: (h, x, z + step, y, c))


def neighbour_slabs(value):
    def up(h, x, z, y, c):
        if c == 0:
            return (h, x, z, y, 1)
        return (h + y, x, z, 1 - y, 0)

    def down(h, x, z, y, c):
        if c == 1:
            return (h, x, z, y, 0)
        return (h + 1 - y, x, z, 1 - y, 1)

    return send(value, up), send(value, down)


def together(*values):
    return lax.optimization_barrier(values)


STEPS = (1, -1, 2)


def piece_places():
    ring = (0, -1, 1, 2)
    offsets = [(0, 0, d) for d in ring] + [(1, d, 0) for d in ring]
    offsets += [(0, s, d) for s in ring[1:] for d in ring]
    offsets += [(1, d, s) for s in ring[1:] for d in ring]
    member = lax.axis_index("member")
    flip, dx, dz = (jnp.array(column, jnp.int32) for column in zip(*offsets))
    y_hi, x, z = member // 16, member // 4 % 4, member % 4
    return ((y_hi + flip) % 2 * 16 + (x + dx + 4) % 4 * 4 + (z + dz + 4) % 4).astype(jnp.int32)


def window_rows(rows):
    count = lax.axis_size("space")
    slab = lax.axis_index("space")
    by_slab = rows.reshape(BATCHES, count, OB * BLK)
    pick = (slab - 1 + jnp.arange(3, dtype=jnp.int32)) % count
    return by_slab[:, pick].reshape(BATCHES, WIN * BLK)


def per_device(
    states, obs_values, obs_weights, obs_cell, op_select, op_table, loc_obs, loc_tile, loc_tiles
):
    obs_cell, op_select = obs_cell[:, 0], op_select[:, 0]
    loc_obs, loc_tile = loc_obs[:, 0], loc_tile[:, 0]
    values, weights = window_rows(obs_values), window_rows(obs_weights)

    loc = jnp.concatenate([loc_obs[0], loc_tile[0]], axis=1).astype(F32)
    loc = jnp.pad(loc, ((0, ROWS - CB_DEV), (0, BLK - 2 * LOC)))
    near = observe_members(states, obs_cell, op_select, op_table, loc)
    far = send(near, lambda h, x, z, y, c: (1 - h, x, z, y, c))
    near, far = together(near, far)
    parts = together(*[along_z(near, d) for d in STEPS], *[along_x(far, d) for d in STEPS])
    near = jnp.concatenate([near, *parts[:3]], axis=0)
    far = jnp.concatenate([far, *parts[3:]], axis=0)
    near, far = together(near, far)
    pieces = [near, far, *[along_x(near, d) for d in STEPS], *[along_z(far, d) for d in STEPS]]
    tiles = weighted_tiles(
        jnp.concatenate([loc_obs[0], loc_obs[1]], axis=0),
        jnp.concatenate([loc_tile[0], loc_tile[1]], axis=0),
        loc_tiles,
        weights,
    )
    *pieces, tiles, states = together(*pieces, tiles, states)
    cells = lax.all_to_all(states, "member", split_axis=1, concat_axis=0, tiled=True)

    observed, raw, loc = assemble(pieces, piece_places())
    loc = loc.reshape(MEMBERS, 8, BLK)[:, :CB_DEV, : 2 * LOC].reshape(MEMBERS * CB_DEV, 2 * LOC)
    loc = loc[obs_cell[1]].astype(jnp.int32)
    before, after = neighbour_slabs(observed)
    tiles_obs = weighted_tiles(loc[:, :LOC], loc[:, LOC:], loc_tiles, weights)
    split_raw = own_gains(raw, observed, tiles_obs, 0, values[:1], "own_gains_observed")
    own = observed
    observed = update(
        raw, split_raw, before, after, tiles_obs, 0, values[:1], "update_observed",
        (op_select, op_table),
    )
    before_next, after_next = neighbour_slabs(observed)
    split = own_gains(cells, own, tiles, 0, values[:1], "own_gains_first")
    cells = update(cells, split, before, after, tiles, 0, values[:1], "update_first")
    split = own_gains(cells, observed, tiles, CELLS, values[1:], "own_gains_second")
    cells = update(
        cells, split, before_next, after_next, tiles, CELLS, values[1:], "update_second"
    )
    return lax.all_to_all(cells, "member", split_axis=0, concat_axis=1, tiled=True)


def solution(mesh):
    placed = (
        P("member", "space"),
        P(),
        P(),
        P(None, "space", None),
        P(None, "space", None),
        P(),
        P(None, "space", "member", None),
        P(None, "space", "member", None),
        P(),
    )
    return jax.shard_map(
        per_device, mesh=mesh, in_specs=placed, out_specs=P("member", "space"), check_vma=False
    )
```

```python
import functools

import jax
import jax.numpy as jnp
from jax import lax
from jax.experimental import pallas as pl
from jax.experimental.pallas import tpu as pltpu
from jax.sharding import PartitionSpec as P

K = 1024
BLK = 128
OB = 4
LOC = 8
BATCHES = 2
MEMBERS = 32
CB_DEV = 6
WIN = 3 * OB
PAD = 16
VMEM_BYTES = 60 * 1024 * 1024

F32 = jnp.float32
BF16 = jnp.bfloat16
PARAMS = pltpu.CompilerParams(vmem_limit_bytes=VMEM_BYTES)


def split_high_low(value):
    high = value.astype(BF16)
    low = (value - high.astype(F32)).astype(BF16)
    return high, low


def dot_nn(a, b):
    return lax.dot_general(a, b, (((1,), (0,)), ((), ())), preferred_element_type=F32)


def dot_nt(a, b, precision=None):
    return lax.dot_general(
        a, b, (((1,), (1,)), ((), ())), preferred_element_type=F32, precision=precision
    )


def observe_kernel(cell_ref, op_ref, *refs):
    first, second, ops = refs[:OB], refs[OB : 2 * OB], refs[2 * OB : 3 * OB]
    loc_ref, out_ref = refs[3 * OB :]
    out_ref[:, 2 * OB * BLK :] = loc_ref[...]
    for o in range(OB):
        out_ref[:, o * BLK : (o + 1) * BLK] = dot_nt(
            first[o][...], ops[o][0], lax.Precision.HIGHEST
        )
        out_ref[:, (OB + o) * BLK : (OB + o + 1) * BLK] = second[o][...]


def observe_members(states, obs_cell, op_select, op_table, loc):
    members = states.shape[0]

    def cells_of(batch, o):
        return pl.BlockSpec((members, BLK), lambda i, cell, op: (0, cell[batch, o]))

    def operator_of(o):
        return pl.BlockSpec((1, BLK, BLK), lambda i, cell, op: (op[0, o], 0, 0))

    width = (2 * OB + 1) * BLK
    whole = pl.BlockSpec((members, width), lambda i, cell, op: (0, 0))
    shape = jax.ShapeDtypeStruct((members, width), F32)
    return pl.pallas_call(
        observe_kernel,
        grid_spec=pltpu.PrefetchScalarGridSpec(
            num_scalar_prefetch=2,
            grid=(1,),
            in_specs=[cells_of(b, o) for b in range(BATCHES) for o in range(OB)]
            + [operator_of(o) for o in range(OB)]
            + [pl.BlockSpec((members, BLK), lambda i, cell, op: (0, 0))],
            out_specs=whole,
        ),
        out_shape=shape,
        compiler_params=PARAMS,
        name="observe",
    )(obs_cell, op_select, *([states] * (2 * OB)), *([op_table] * OB), loc)


def tiles_kernel(obs_ref, tile_ref, tiles_ref, weights_ref, out_ref):
    n = pl.program_id(0)
    out_ref[...] = jnp.zeros_like(out_ref)
    for l in range(LOC):
        cols = pl.ds(pl.multiple_of(obs_ref[n, l] * BLK, BLK), BLK)
        scale = weights_ref[0, :, cols] * (-0.5 / (K - 1))
        out_ref[:, cols] += tiles_ref[tile_ref[n, l]] * scale


def weighted_tiles(loc_obs, loc_tile, loc_tiles, weights):
    blocks = loc_obs.shape[0]
    return pl.pallas_call(
        tiles_kernel,
        grid_spec=pltpu.PrefetchScalarGridSpec(
            num_scalar_prefetch=2,
            grid=(blocks,),
            in_specs=[
                pl.BlockSpec(loc_tiles.shape, lambda n, a, b: (0, 0, 0)),
                pl.BlockSpec(
                    (1, 1, WIN * BLK),
                    lambda n, a, b: (jnp.where((n >= CB_DEV) & (n < 2 * CB_DEV), 1, 0), 0, 0),
                ),
            ],
            out_specs=pl.BlockSpec((BLK, WIN * BLK), lambda n, a, b: (n, 0)),
        ),
        out_shape=jax.ShapeDtypeStruct((blocks * BLK, WIN * BLK), F32),
        compiler_params=PARAMS,
        cost_estimate=pl.CostEstimate(flops=1 << 22, bytes_accessed=14 << 20, transcendentals=0),
        name="weighted_tiles",
    )(loc_obs, loc_tile, loc_tiles, weights.reshape(BATCHES, 1, WIN * BLK))


CHUNK = 2 * BLK
SLAB = OB * BLK
ROWS = 32
ANY = pl.BlockSpec(memory_space=pl.ANY)
SMEM = pl.BlockSpec(memory_space=pltpu.SMEM)
VMEM = pl.BlockSpec(memory_space=pltpu.VMEM)


def chunk(number):
    return slice(number * CHUNK, (number + 1) * CHUNK)


def split_observed(y_ref, src, dst, values_ref, yh, yl):
    y = y_ref[:, chunk(src)]
    mean = jnp.sum(y, axis=0, keepdims=True) * (1.0 / K)
    yh[0:K, chunk(dst)], yl[0:K, chunk(dst)] = split_high_low(y - mean)
    shift = jnp.broadcast_to(-2.0 * (values_ref[:, chunk(dst)] - mean), (PAD, CHUNK))
    yh[K : K + PAD, chunk(dst)], yl[K : K + PAD, chunk(dst)] = split_high_low(shift)


def split_cells(x_ref, col0, nb, xh, xl):
    for n in range(nb):
        x = x_ref[:, col0 + n * BLK : col0 + (n + 1) * BLK]
        anom = x - jnp.sum(x, axis=0, keepdims=True) * (1.0 / K)
        rows = slice(n * BLK, (n + 1) * BLK)
        xh[rows, :], xl[rows, :] = split_high_low(anom.T)


def gains(cols, tile_cols, tiles_ref, xh, xl, yh, yl, gh, gl):
    high, low = yh[0:K, cols], yl[0:K, cols]
    cov = dot_nn(xh[...], high) + dot_nn(xh[...], low) + dot_nn(xl[...], high)
    gh[:, cols], gl[:, cols] = split_high_low(cov * tiles_ref[:, tile_cols])


def increment(number, yh, yl, gh, gl):
    high, low = gh[chunk(number), :], gl[chunk(number), :]
    inc = dot_nt(yh[...], high) + dot_nt(yh[...], low) + dot_nt(yl[...], high)
    return inc[0:K] + inc[K : K + 1]


def bf16_pair(rows, cols):
    return [jax.ShapeDtypeStruct((rows, cols), BF16)] * 2


def vmem_pair(rows, cols):
    return [pltpu.VMEM((rows, cols), BF16)] * 2


def copies(sems, pairs):
    out = [pltpu.make_async_copy(src, dst, sems.at[i]) for i, (src, dst) in enumerate(pairs)]
    for copy in out:
        copy.start()
    return out


CELLS = CB_DEV * BLK
WINDOW = WIN * BLK
OWN = slice(SLAB, 2 * SLAB)


def own_gains_kernel(
    row0, values_ref, x_in, own_in, t_in,
    xh_out, xl_out, yh_out, yl_out, gh_out, gl_out,
    x, own, tiles, xh, xl, yh, yl, gh, gl, sems,
):
    cells = x.shape[1]
    x_load, own_load, t_load = copies(
        sems, [(x_in, x), (own_in, own), (t_in.at[row0 : row0 + cells, OWN], tiles)]
    )
    x_load.wait()
    split_cells(x, 0, cells // BLK, xh, xl)
    stores = []

    def store(source, target):
        stores.append(pltpu.make_async_copy(source, target, sems.at[3 + len(stores)]))
        stores[-1].start()

    store(xh, xh_out)
    store(xl, xl_out)
    own_load.wait()
    t_load.wait()
    for number in range(SLAB // CHUNK):
        split_observed(own, number, number, values_ref, yh, yl)
        gains(chunk(number), chunk(number), tiles, xh, xl, yh, yl, gh, gl)
    store(yh, yh_out)
    store(yl, yl_out)
    store(gh, gh_out)
    store(gl, gl_out)
    for copy in stores:
        copy.wait()


def own_gains(cells, own, tiles, row0, values, name):
    count = cells.shape[1]
    return pl.pallas_call(
        functools.partial(own_gains_kernel, row0),
        in_specs=[VMEM] + [ANY] * 3,
        out_specs=[ANY] * 6,
        out_shape=bf16_pair(count, K) + bf16_pair(K + PAD, SLAB) + bf16_pair(count, SLAB),
        scratch_shapes=[
            pltpu.VMEM((K, count), F32),
            pltpu.VMEM((K, SLAB), F32),
            pltpu.VMEM((count, SLAB), F32),
        ]
        + vmem_pair(count, K)
        + vmem_pair(K + PAD, SLAB)
        + vmem_pair(count, SLAB)
        + [pltpu.SemaphoreType.DMA((9,))],
        compiler_params=PARAMS,
        cost_estimate=pl.CostEstimate(
            flops=6 * K * count * SLAB, bytes_accessed=14 << 20, transcendentals=0
        ),
        name=name,
    )(values[:, OWN], cells, own, tiles)


def update_kernel(
    row0, observing, values_ref,
    x_in, xh_in, xl_in, yh_in, yl_in, gh_in, gl_in, before_in, after_in, t_in, *refs,
):
    if observing:
        op_ref, ops, x_out, oph, opl, *refs = refs
    else:
        x_out, *refs = refs
    x, xh, xl, yh, yl, gh, gl, y, tiles, sems = refs
    cells = x.shape[1]
    loads = copies(
        sems,
        [
            (before_in, y.at[:, 0:SLAB]),
            (xh_in, xh),
            (xl_in, xl),
            (t_in.at[row0 : row0 + cells, :], tiles),
            (after_in, y.at[:, SLAB : 2 * SLAB]),
            (yh_in, yh.at[:, OWN]),
            (yl_in, yl.at[:, OWN]),
            (gh_in, gh.at[:, OWN]),
            (gl_in, gl.at[:, OWN]),
            (x_in, x),
        ],
    )
    count = len(loads)
    per = SLAB // CHUNK
    for load in loads[:4]:
        load.wait()
    for number in range(per):
        split_observed(y, number, number, values_ref, yh, yl)
        gains(chunk(number), chunk(number), tiles, xh, xl, yh, yl, gh, gl)
    loads[4].wait()
    for number in range(per):
        split_observed(y, per + number, 2 * per + number, values_ref, yh, yl)
        cols = chunk(2 * per + number)
        gains(cols, cols, tiles, xh, xl, yh, yl, gh, gl)
    for load in loads[5:]:
        load.wait()
    stores = []

    def store(source, target):
        stores.append(pltpu.make_async_copy(source, target, sems.at[count + len(stores)]))
        stores[-1].start()

    for number in range(cells // CHUNK):
        x[:, chunk(number)] += increment(number, yh, yl, gh, gl)
        if not observing:
            store(x.at[:, chunk(number)], x_out.at[:, chunk(number)])
    if observing:
        zero = jnp.zeros((BLK, BLK), F32)
        for number in range(cells // CHUNK):
            first, second = ops[op_ref[1, 2 * number]], ops[op_ref[1, 2 * number + 1]]
            pair = jnp.concatenate(
                [jnp.concatenate([first, zero], 1), jnp.concatenate([zero, second], 1)], 0
            )
            oph[chunk(number), :], opl[chunk(number), :] = split_high_low(pair)

        @pl.loop(0, K // CHUNK)
        def _(part):
            rows = pl.ds(pl.multiple_of(part * CHUNK, CHUNK), CHUNK)
            for number in range(cells // CHUNK):
                high, low = split_high_low(x[rows, chunk(number)])
                op_high, op_low = oph[chunk(number), :], opl[chunk(number), :]
                x[rows, chunk(number)] = (
                    dot_nt(high, op_high) + dot_nt(high, op_low) + dot_nt(low, op_high)
                )

        store(x, x_out)
    for copy in stores:
        copy.wait()


def update(cells, split, before, after, tiles, row0, values, name, operators=None):
    count = cells.shape[1]
    observing = operators is not None
    return pl.pallas_call(
        functools.partial(update_kernel, row0, observing),
        in_specs=[VMEM] + [ANY] * 10 + ([SMEM, VMEM] if observing else []),
        out_specs=ANY,
        out_shape=jax.ShapeDtypeStruct((K, count), F32),
        scratch_shapes=(vmem_pair(count, CHUNK) if observing else [])
        + [pltpu.VMEM((K, count), F32)]
        + vmem_pair(count, K)
        + vmem_pair(K + PAD, WINDOW)
        + vmem_pair(count, WINDOW)
        + [
            pltpu.VMEM((K, 2 * SLAB), F32),
            pltpu.VMEM((count, WINDOW), F32),
            pltpu.SemaphoreType.DMA((13,)),
        ],
        compiler_params=PARAMS,
        cost_estimate=pl.CostEstimate(
            flops=10 * K * count * WINDOW, bytes_accessed=25 << 20, transcendentals=0
        ),
        name=name,
    )(values, cells, *split, before, after, tiles, *(operators or ()))


def assemble_kernel(sizes, at_ref, *refs):
    count = len(sizes)
    pieces, (observed, raw, loc) = refs[:count], refs[count:]
    place = 0
    for piece, size in zip(pieces, sizes):
        for q in range(size):
            part = slice(q * ROWS, (q + 1) * ROWS)
            rows = pl.ds(pl.multiple_of(at_ref[place] * ROWS, ROWS), ROWS)
            observed[rows, :] = piece[part, 0:SLAB]
            raw[rows, :] = piece[part, SLAB : 2 * SLAB]
            rows = pl.ds(pl.multiple_of(at_ref[place] * 8, 8), 8)
            loc[rows, :] = piece[q * ROWS : q * ROWS + 8, 2 * SLAB : 2 * SLAB + BLK]
            place += 1


def assemble(pieces, places):
    sizes = tuple(piece.shape[0] // ROWS for piece in pieces)
    return pl.pallas_call(
        functools.partial(assemble_kernel, sizes),
        in_specs=[SMEM] + [VMEM] * len(pieces),
        out_specs=[VMEM] * 3,
        out_shape=[jax.ShapeDtypeStruct((K, SLAB), F32)] * 2
        + [jax.ShapeDtypeStruct((8 * MEMBERS, BLK), F32)],
        compiler_params=PARAMS,
        cost_estimate=pl.CostEstimate(flops=0, bytes_accessed=8 << 20, transcendentals=0),
        name="assemble",
    )(places, *pieces)


BOTH = ("member", "space")


def send(value, target):
    pairs = []
    for index in range(128):
        member, slab = index // 4, index % 4
        y_hi, x, z = target(member // 16, member // 4 % 4, member % 4, slab // 2, slab % 2)[:3]
        y_lo, core = target(member // 16, member // 4 % 4, member % 4, slab // 2, slab % 2)[3:]
        pairs.append((index, (y_hi % 2 * 16 + x % 4 * 4 + z % 4) * 4 + y_lo % 2 * 2 + core % 2))
    return lax.ppermute(value, BOTH, pairs)


def along_x(value, step):
    return send(value, lambda h, x, z, y, c: (h, x + step, z, y, c))


def along_z(value, step):
    return send(value, lambda h, x, z, y, c: (h, x, z + step, y, c))


def neighbour_slabs(value):
    def up(h, x, z, y, c):
        if c == 0:
            return (h, x, z, y, 1)
        return (h + y, x, z, 1 - y, 0)

    def down(h, x, z, y, c):
        if c == 1:
            return (h, x, z, y, 0)
        return (h + 1 - y, x, z, 1 - y, 1)

    return send(value, up), send(value, down)


def together(*values):
    return lax.optimization_barrier(values)


STEPS = (1, -1, 2)


def piece_places():
    ring = (0, -1, 1, 2)
    offsets = [(0, 0, d) for d in ring] + [(1, d, 0) for d in ring]
    offsets += [(0, s, d) for s in ring[1:] for d in ring]
    offsets += [(1, d, s) for s in ring[1:] for d in ring]
    member = lax.axis_index("member")
    flip, dx, dz = (jnp.array(column, jnp.int32) for column in zip(*offsets))
    y_hi, x, z = member // 16, member // 4 % 4, member % 4
    return ((y_hi + flip) % 2 * 16 + (x + dx + 4) % 4 * 4 + (z + dz + 4) % 4).astype(jnp.int32)


def window_rows(rows):
    count = lax.axis_size("space")
    slab = lax.axis_index("space")
    by_slab = rows.reshape(BATCHES, count, OB * BLK)
    pick = (slab - 1 + jnp.arange(3, dtype=jnp.int32)) % count
    return by_slab[:, pick].reshape(BATCHES, WIN * BLK)


def per_device(
    states, obs_values, obs_weights, obs_cell, op_select, op_table, loc_obs, loc_tile, loc_tiles
):
    obs_cell, op_select = obs_cell[:, 0], op_select[:, 0]
    loc_obs, loc_tile = loc_obs[:, 0], loc_tile[:, 0]
    values, weights = window_rows(obs_values), window_rows(obs_weights)

    loc = jnp.concatenate([loc_obs[0], loc_tile[0]], axis=1).astype(F32)
    loc = jnp.pad(loc, ((0, ROWS - CB_DEV), (0, BLK - 2 * LOC)))
    near = observe_members(states, obs_cell, op_select, op_table, loc)
    far = send(near, lambda h, x, z, y, c: (1 - h, x, z, y, c))
    near, far = together(near, far)
    parts = together(*[along_z(near, d) for d in STEPS], *[along_x(far, d) for d in STEPS])
    near = jnp.concatenate([near, *parts[:3]], axis=0)
    far = jnp.concatenate([far, *parts[3:]], axis=0)
    near, far = together(near, far)
    pieces = [near, far, *[along_x(near, d) for d in STEPS], *[along_z(far, d) for d in STEPS]]
    *pieces, states = together(*pieces, states)
    cells = lax.all_to_all(states, "member", split_axis=1, concat_axis=0, tiled=True)

    observed, raw, loc = assemble(pieces, piece_places())
    loc = loc.reshape(MEMBERS, 8, BLK)[:, :CB_DEV, : 2 * LOC].reshape(MEMBERS * CB_DEV, 2 * LOC)
    loc = loc[obs_cell[1]].astype(jnp.int32)
    observed, loc_tiles = together(observed, loc_tiles)
    before, after = neighbour_slabs(observed)
    tiles = weighted_tiles(
        jnp.concatenate([loc_obs[0], loc_obs[1]], axis=0),
        jnp.concatenate([loc_tile[0], loc_tile[1]], axis=0),
        loc_tiles,
        weights,
    )
    tiles_obs = weighted_tiles(loc[:, :LOC], loc[:, LOC:], loc_tiles, weights)
    split_raw = own_gains(raw, observed, tiles_obs, 0, values[:1], "own_gains_observed")
    own = observed
    before, after, tiles, *split_raw = together(before, after, tiles, *split_raw)
    observed = update(
        raw, split_raw, before, after, tiles_obs, 0, values[:1], "update_observed",
        (op_select, op_table),
    )
    before_next, after_next = neighbour_slabs(observed)
    split = own_gains(cells, own, tiles, 0, values[:1], "own_gains_first")
    cells = update(cells, split, before, after, tiles, 0, values[:1], "update_first")
    split = own_gains(cells, observed, tiles, CELLS, values[1:], "own_gains_second")
    cells = update(
        cells, split, before_next, after_next, tiles, CELLS, values[1:], "update_second"
    )
    return lax.all_to_all(cells, "member", split_axis=0, concat_axis=1, tiled=True)


def solution(mesh):
    placed = (
        P("member", "space"),
        P(),
        P(),
        P(None, "space", None),
        P(None, "space", None),
        P(),
        P(None, "space", "member", None),
        P(None, "space", "member", None),
        P(),
    )
    return jax.shard_map(
        per_device, mesh=mesh, in_specs=placed, out_specs=P("member", "space"), check_vma=False
    )
```

```python
import functools

import jax
import jax.numpy as jnp
from jax import lax
from jax.experimental import pallas as pl
from jax.experimental.pallas import tpu as pltpu
from jax.sharding import PartitionSpec as P

K = 1024
BLK = 128
OB = 4
LOC = 8
BATCHES = 2
MEMBERS = 32
CB_DEV = 6
WIN = 3 * OB
PAD = 16
VMEM_BYTES = 60 * 1024 * 1024

F32 = jnp.float32
BF16 = jnp.bfloat16
PARAMS = pltpu.CompilerParams(vmem_limit_bytes=VMEM_BYTES)


def split_high_low(value):
    high = value.astype(BF16)
    low = (value - high.astype(F32)).astype(BF16)
    return high, low


def dot_nn(a, b):
    return lax.dot_general(a, b, (((1,), (0,)), ((), ())), preferred_element_type=F32)


def dot_nt(a, b, precision=None):
    return lax.dot_general(
        a, b, (((1,), (1,)), ((), ())), preferred_element_type=F32, precision=precision
    )


def observe_kernel(cell_ref, op_ref, *refs):
    first, second, ops = refs[:OB], refs[OB : 2 * OB], refs[2 * OB : 3 * OB]
    loc_ref, out_ref = refs[3 * OB :]
    out_ref[:, 2 * OB * BLK :] = loc_ref[...]
    for o in range(OB):
        out_ref[:, o * BLK : (o + 1) * BLK] = dot_nt(
            first[o][...], ops[o][0], lax.Precision.HIGHEST
        )
        out_ref[:, (OB + o) * BLK : (OB + o + 1) * BLK] = second[o][...]


def observe_members(states, obs_cell, op_select, op_table, loc):
    members = states.shape[0]

    def cells_of(batch, o):
        return pl.BlockSpec((members, BLK), lambda i, cell, op: (0, cell[batch, o]))

    def operator_of(o):
        return pl.BlockSpec((1, BLK, BLK), lambda i, cell, op: (op[0, o], 0, 0))

    width = (2 * OB + 1) * BLK
    whole = pl.BlockSpec((members, width), lambda i, cell, op: (0, 0))
    shape = jax.ShapeDtypeStruct((members, width), F32)
    return pl.pallas_call(
        observe_kernel,
        grid_spec=pltpu.PrefetchScalarGridSpec(
            num_scalar_prefetch=2,
            grid=(1,),
            in_specs=[cells_of(b, o) for b in range(BATCHES) for o in range(OB)]
            + [operator_of(o) for o in range(OB)]
            + [pl.BlockSpec((members, BLK), lambda i, cell, op: (0, 0))],
            out_specs=whole,
        ),
        out_shape=shape,
        compiler_params=PARAMS,
        name="observe",
    )(obs_cell, op_select, *([states] * (2 * OB)), *([op_table] * OB), loc)


def tiles_kernel(obs_ref, tile_ref, tiles_ref, weights_ref, out_ref):
    n = pl.program_id(0)
    out_ref[...] = jnp.zeros_like(out_ref)
    for l in range(LOC):
        cols = pl.ds(pl.multiple_of(obs_ref[n, l] * BLK, BLK), BLK)
        scale = weights_ref[0, :, cols] * (-0.5 / (K - 1))
        out_ref[:, cols] += tiles_ref[tile_ref[n, l]] * scale


def weighted_tiles(loc_obs, loc_tile, loc_tiles, weights):
    blocks = loc_obs.shape[0]
    return pl.pallas_call(
        tiles_kernel,
        grid_spec=pltpu.PrefetchScalarGridSpec(
            num_scalar_prefetch=2,
            grid=(blocks,),
            in_specs=[
                pl.BlockSpec(loc_tiles.shape, lambda n, a, b: (0, 0, 0)),
                pl.BlockSpec(
                    (1, 1, WIN * BLK),
                    lambda n, a, b: (jnp.where((n >= CB_DEV) & (n < 2 * CB_DEV), 1, 0), 0, 0),
                ),
            ],
            out_specs=pl.BlockSpec((BLK, WIN * BLK), lambda n, a, b: (n, 0)),
        ),
        out_shape=jax.ShapeDtypeStruct((blocks * BLK, WIN * BLK), F32),
        compiler_params=PARAMS,
        cost_estimate=pl.CostEstimate(flops=1 << 22, bytes_accessed=14 << 20, transcendentals=0),
        name="weighted_tiles",
    )(loc_obs, loc_tile, loc_tiles, weights.reshape(BATCHES, 1, WIN * BLK))


CHUNK = 2 * BLK
SLAB = OB * BLK
ROWS = 32
ANY = pl.BlockSpec(memory_space=pl.ANY)
SMEM = pl.BlockSpec(memory_space=pltpu.SMEM)
VMEM = pl.BlockSpec(memory_space=pltpu.VMEM)


def chunk(number):
    return slice(number * CHUNK, (number + 1) * CHUNK)


def split_observed(y_ref, src, dst, values_ref, yh, yl):
    y = y_ref[:, chunk(src)]
    mean = jnp.sum(y, axis=0, keepdims=True) * (1.0 / K)
    yh[0:K, chunk(dst)], yl[0:K, chunk(dst)] = split_high_low(y - mean)
    shift = jnp.broadcast_to(-2.0 * (values_ref[:, chunk(dst)] - mean), (PAD, CHUNK))
    yh[K : K + PAD, chunk(dst)], yl[K : K + PAD, chunk(dst)] = split_high_low(shift)


def split_cells(x_ref, col0, nb, xh, xl):
    for n in range(nb):
        x = x_ref[:, col0 + n * BLK : col0 + (n + 1) * BLK]
        anom = x - jnp.sum(x, axis=0, keepdims=True) * (1.0 / K)
        rows = slice(n * BLK, (n + 1) * BLK)
        xh[rows, :], xl[rows, :] = split_high_low(anom.T)


def gains(cols, tile_cols, tiles_ref, xh, xl, yh, yl, gh, gl):
    high, low = yh[0:K, cols], yl[0:K, cols]
    cov = dot_nn(xh[...], high) + dot_nn(xh[...], low) + dot_nn(xl[...], high)
    gh[:, cols], gl[:, cols] = split_high_low(cov * tiles_ref[:, tile_cols])


def increment(number, yh, yl, gh, gl):
    high, low = gh[chunk(number), :], gl[chunk(number), :]
    inc = dot_nt(yh[...], high) + dot_nt(yh[...], low) + dot_nt(yl[...], high)
    return inc[0:K] + inc[K : K + 1]


def bf16_pair(rows, cols):
    return [jax.ShapeDtypeStruct((rows, cols), BF16)] * 2


def vmem_pair(rows, cols):
    return [pltpu.VMEM((rows, cols), BF16)] * 2


def copies(sems, pairs):
    out = [pltpu.make_async_copy(src, dst, sems.at[i]) for i, (src, dst) in enumerate(pairs)]
    for copy in out:
        copy.start()
    return out


CELLS = CB_DEV * BLK
WINDOW = WIN * BLK
OWN = slice(SLAB, 2 * SLAB)


def own_gains_kernel(
    row0, values_ref, x_in, own_in, t_in,
    xh_out, xl_out, yh_out, yl_out, gh_out, gl_out,
    x, own, tiles, xh, xl, yh, yl, gh, gl, sems,
):
    cells = x.shape[1]
    x_load, own_load, t_load = copies(
        sems, [(x_in, x), (own_in, own), (t_in.at[row0 : row0 + cells, OWN], tiles)]
    )
    x_load.wait()
    split_cells(x, 0, cells // BLK, xh, xl)
    stores = []

    def store(source, target):
        stores.append(pltpu.make_async_copy(source, target, sems.at[3 + len(stores)]))
        stores[-1].start()

    store(xh, xh_out)
    store(xl, xl_out)
    own_load.wait()
    t_load.wait()
    for number in range(SLAB // CHUNK):
        split_observed(own, number, number, values_ref, yh, yl)
        gains(chunk(number), chunk(number), tiles, xh, xl, yh, yl, gh, gl)
    store(yh, yh_out)
    store(yl, yl_out)
    store(gh, gh_out)
    store(gl, gl_out)
    for copy in stores:
        copy.wait()


def own_gains(cells, own, tiles, row0, values, name):
    count = cells.shape[1]
    return pl.pallas_call(
        functools.partial(own_gains_kernel, row0),
        in_specs=[VMEM] + [ANY] * 3,
        out_specs=[ANY] * 6,
        out_shape=bf16_pair(count, K) + bf16_pair(K + PAD, SLAB) + bf16_pair(count, SLAB),
        scratch_shapes=[
            pltpu.VMEM((K, count), F32),
            pltpu.VMEM((K, SLAB), F32),
            pltpu.VMEM((count, SLAB), F32),
        ]
        + vmem_pair(count, K)
        + vmem_pair(K + PAD, SLAB)
        + vmem_pair(count, SLAB)
        + [pltpu.SemaphoreType.DMA((9,))],
        compiler_params=PARAMS,
        cost_estimate=pl.CostEstimate(
            flops=6 * K * count * SLAB, bytes_accessed=14 << 20, transcendentals=0
        ),
        name=name,
    )(values[:, OWN], cells, own, tiles)


def update_kernel(
    row0, observing, values_ref,
    x_in, xh_in, xl_in, yh_in, yl_in, gh_in, gl_in, before_in, after_in, t_in, *refs,
):
    if observing:
        op_ref, ops, x_out, oph, opl, *refs = refs
    else:
        x_out, *refs = refs
    x, xh, xl, yh, yl, gh, gl, y, tiles, sems = refs
    cells = x.shape[1]
    loads = copies(
        sems,
        [
            (before_in, y.at[:, 0:SLAB]),
            (xh_in, xh),
            (xl_in, xl),
            (t_in.at[row0 : row0 + cells, :], tiles),
            (after_in, y.at[:, SLAB : 2 * SLAB]),
            (yh_in, yh.at[:, OWN]),
            (yl_in, yl.at[:, OWN]),
            (gh_in, gh.at[:, OWN]),
            (gl_in, gl.at[:, OWN]),
            (x_in, x),
        ],
    )
    count = len(loads)
    per = SLAB // CHUNK
    for load in loads[:4]:
        load.wait()
    for number in range(per):
        split_observed(y, number, number, values_ref, yh, yl)
        gains(chunk(number), chunk(number), tiles, xh, xl, yh, yl, gh, gl)
    loads[4].wait()
    for number in range(per):
        split_observed(y, per + number, 2 * per + number, values_ref, yh, yl)
        cols = chunk(2 * per + number)
        gains(cols, cols, tiles, xh, xl, yh, yl, gh, gl)
    for load in loads[5:]:
        load.wait()
    stores = []

    def store(source, target):
        stores.append(pltpu.make_async_copy(source, target, sems.at[count + len(stores)]))
        stores[-1].start()

    for number in range(cells // CHUNK):
        x[:, chunk(number)] += increment(number, yh, yl, gh, gl)
        if not observing:
            store(x.at[:, chunk(number)], x_out.at[:, chunk(number)])
    if observing:
        zero = jnp.zeros((BLK, BLK), F32)
        for number in range(cells // CHUNK):
            first, second = ops[op_ref[1, 2 * number]], ops[op_ref[1, 2 * number + 1]]
            pair = jnp.concatenate(
                [jnp.concatenate([first, zero], 1), jnp.concatenate([zero, second], 1)], 0
            )
            oph[chunk(number), :], opl[chunk(number), :] = split_high_low(pair)

        @pl.loop(0, K // CHUNK)
        def _(part):
            rows = pl.ds(pl.multiple_of(part * CHUNK, CHUNK), CHUNK)
            for number in range(cells // CHUNK):
                high, low = split_high_low(x[rows, chunk(number)])
                op_high, op_low = oph[chunk(number), :], opl[chunk(number), :]
                x[rows, chunk(number)] = (
                    dot_nt(high, op_high) + dot_nt(high, op_low) + dot_nt(low, op_high)
                )

        store(x, x_out)
    for copy in stores:
        copy.wait()


def update(cells, split, before, after, tiles, row0, values, name, operators=None):
    count = cells.shape[1]
    observing = operators is not None
    return pl.pallas_call(
        functools.partial(update_kernel, row0, observing),
        in_specs=[VMEM] + [ANY] * 10 + ([SMEM, VMEM] if observing else []),
        out_specs=ANY,
        out_shape=jax.ShapeDtypeStruct((K, count), F32),
        scratch_shapes=(vmem_pair(count, CHUNK) if observing else [])
        + [pltpu.VMEM((K, count), F32)]
        + vmem_pair(count, K)
        + vmem_pair(K + PAD, WINDOW)
        + vmem_pair(count, WINDOW)
        + [
            pltpu.VMEM((K, 2 * SLAB), F32),
            pltpu.VMEM((count, WINDOW), F32),
            pltpu.SemaphoreType.DMA((13,)),
        ],
        compiler_params=PARAMS,
        cost_estimate=pl.CostEstimate(
            flops=10 * K * count * WINDOW, bytes_accessed=25 << 20, transcendentals=0
        ),
        name=name,
    )(values, cells, *split, before, after, tiles, *(operators or ()))


def assemble_kernel(sizes, at_ref, *refs):
    count = len(sizes)
    pieces, (observed, raw, loc) = refs[:count], refs[count:]
    place = 0
    for piece, size in zip(pieces, sizes):
        for q in range(size):
            part = slice(q * ROWS, (q + 1) * ROWS)
            rows = pl.ds(pl.multiple_of(at_ref[place] * ROWS, ROWS), ROWS)
            observed[rows, :] = piece[part, 0:SLAB]
            raw[rows, :] = piece[part, SLAB : 2 * SLAB]
            rows = pl.ds(pl.multiple_of(at_ref[place] * 8, 8), 8)
            loc[rows, :] = piece[q * ROWS : q * ROWS + 8, 2 * SLAB : 2 * SLAB + BLK]
            place += 1


def assemble(pieces, places):
    sizes = tuple(piece.shape[0] // ROWS for piece in pieces)
    return pl.pallas_call(
        functools.partial(assemble_kernel, sizes),
        in_specs=[SMEM] + [VMEM] * len(pieces),
        out_specs=[VMEM] * 3,
        out_shape=[jax.ShapeDtypeStruct((K, SLAB), F32)] * 2
        + [jax.ShapeDtypeStruct((8 * MEMBERS, BLK), F32)],
        compiler_params=PARAMS,
        cost_estimate=pl.CostEstimate(flops=0, bytes_accessed=8 << 20, transcendentals=0),
        name="assemble",
    )(places, *pieces)


BOTH = ("member", "space")


def send(value, target):
    pairs = []
    for index in range(128):
        member, slab = index // 4, index % 4
        y_hi, x, z = target(member // 16, member // 4 % 4, member % 4, slab // 2, slab % 2)[:3]
        y_lo, core = target(member // 16, member // 4 % 4, member % 4, slab // 2, slab % 2)[3:]
        pairs.append((index, (y_hi % 2 * 16 + x % 4 * 4 + z % 4) * 4 + y_lo % 2 * 2 + core % 2))
    return lax.ppermute(value, BOTH, pairs)


def along_x(value, step):
    return send(value, lambda h, x, z, y, c: (h, x + step, z, y, c))


def along_z(value, step):
    return send(value, lambda h, x, z, y, c: (h, x, z + step, y, c))


def neighbour_slabs(value):
    def up(h, x, z, y, c):
        if c == 0:
            return (h, x, z, y, 1)
        return (h + y, x, z, 1 - y, 0)

    def down(h, x, z, y, c):
        if c == 1:
            return (h, x, z, y, 0)
        return (h + 1 - y, x, z, 1 - y, 1)

    return send(value, up), send(value, down)


def together(*values):
    return lax.optimization_barrier(values)


STEPS = (1, -1, 2)


def piece_places():
    ring = (0, -1, 1, 2)
    offsets = [(0, 0, d) for d in ring] + [(1, d, 0) for d in ring]
    offsets += [(0, s, d) for s in ring[1:] for d in ring]
    offsets += [(1, d, s) for s in ring[1:] for d in ring]
    member = lax.axis_index("member")
    flip, dx, dz = (jnp.array(column, jnp.int32) for column in zip(*offsets))
    y_hi, x, z = member // 16, member // 4 % 4, member % 4
    return ((y_hi + flip) % 2 * 16 + (x + dx + 4) % 4 * 4 + (z + dz + 4) % 4).astype(jnp.int32)


def window_rows(rows):
    count = lax.axis_size("space")
    slab = lax.axis_index("space")
    by_slab = rows.reshape(BATCHES, count, OB * BLK)
    pick = (slab - 1 + jnp.arange(3, dtype=jnp.int32)) % count
    return by_slab[:, pick].reshape(BATCHES, WIN * BLK)


def per_device(
    states, obs_values, obs_weights, obs_cell, op_select, op_table, loc_obs, loc_tile, loc_tiles
):
    obs_cell, op_select = obs_cell[:, 0], op_select[:, 0]
    loc_obs, loc_tile = loc_obs[:, 0], loc_tile[:, 0]
    values, weights = window_rows(obs_values), window_rows(obs_weights)

    loc = jnp.concatenate([loc_obs[0], loc_tile[0]], axis=1).astype(F32)
    loc = jnp.pad(loc, ((0, ROWS - CB_DEV), (0, BLK - 2 * LOC)))
    near = observe_members(states, obs_cell, op_select, op_table, loc)
    far = send(near, lambda h, x, z, y, c: (1 - h, x, z, y, c))
    near, far = together(near, far)
    parts = together(*[along_z(near, d) for d in STEPS], *[along_x(far, d) for d in STEPS])
    near = jnp.concatenate([near, *parts[:3]], axis=0)
    far = jnp.concatenate([far, *parts[3:]], axis=0)
    near, far, states = together(near, far, states)
    pieces = [near, far, *[along_x(near, d) for d in STEPS], *[along_z(far, d) for d in STEPS]]
    cells = lax.all_to_all(states, "member", split_axis=1, concat_axis=0, tiled=True)
    *pieces, cells = together(*pieces, cells)

    observed, raw, loc = assemble(pieces, piece_places())
    loc = loc.reshape(MEMBERS, 8, BLK)[:, :CB_DEV, : 2 * LOC].reshape(MEMBERS * CB_DEV, 2 * LOC)
    loc = loc[obs_cell[1]].astype(jnp.int32)
    observed, loc_tiles = together(observed, loc_tiles)
    before, after = neighbour_slabs(observed)
    tiles = weighted_tiles(
        jnp.concatenate([loc_obs[0], loc_obs[1]], axis=0),
        jnp.concatenate([loc_tile[0], loc_tile[1]], axis=0),
        loc_tiles,
        weights,
    )
    tiles_obs = weighted_tiles(loc[:, :LOC], loc[:, LOC:], loc_tiles, weights)
    split_raw = own_gains(raw, observed, tiles_obs, 0, values[:1], "own_gains_observed")
    split = own_gains(cells, observed, tiles, 0, values[:1], "own_gains_first")
    before, after, tiles, *both = together(before, after, tiles, *split_raw, *split)
    split_raw, split = both[:6], both[6:]
    observed = update(
        raw, split_raw, before, after, tiles_obs, 0, values[:1], "update_observed",
        (op_select, op_table),
    )
    before_next, after_next = neighbour_slabs(observed)
    cells = update(cells, split, before, after, tiles, 0, values[:1], "update_first")
    split = own_gains(cells, observed, tiles, CELLS, values[1:], "own_gains_second")
    cells = update(
        cells, split, before_next, after_next, tiles, CELLS, values[1:], "update_second"
    )
    return lax.all_to_all(cells, "member", split_axis=0, concat_axis=1, tiled=True)


def solution(mesh):
    placed = (
        P("member", "space"),
        P(),
        P(),
        P(None, "space", None),
        P(None, "space", None),
        P(),
        P(None, "space", "member", None),
        P(None, "space", "member", None),
        P(),
    )
    return jax.shard_map(
        per_device, mesh=mesh, in_specs=placed, out_specs=P("member", "space"), check_vma=False
    )
```
